1024 devices in a mesh: gx: 64 (over y, z), gy: 16 (over x, core).
Axes of the slice: x: 8, y: 8, z: 8, core: 2. Of those that a mesh axis runs over, the one named last changes fastest.
Arguments:
- features: bfloat16 [8, 64, 512, 2048], P(None, None, 'gx', 'gy'), may hold values from -6 to 6
- head_weight: bfloat16 [6, 64], replicated, may hold values from -0.75 to 0.75
- head_bias: float32 [6], replicated, may hold values from -1 to 1
- probs: float32 [8, 8, 512, 2048], P(None, None, 'gx', 'gy'), may hold values from 0 to 1
- cotangent: float32 [8, 8, 512, 2048], P(None, None, 'gx', 'gy'), may hold values from -12 to 12
Outputs:
- grad_probs: float32 [8, 8, 512, 2048], P(None, None, 'gx', 'gy')
- grad_weight: float32 [6, 64], replicated
- grad_bias: float32 [6], replicated
The draws below stay inside these ranges and needn't reach their ends.
All inputs are finite; a program needn't handle non-finite values.
Results may differ from the reference program's by a relative error of at most 0.0027.
Values sent between devices are 32-bit elements; how exact they have to be, the bound alone decides.
A program may use at most 32 MiB of HBM per device.

```python
import math
import jax
import jax.numpy as jnp
from jax import lax

C = 8
F = 64
ZS = 8
ITERS = 3
NX = 512
NY = 2048


def draw_cotangent(key, part):
    first, second = jax.random.split(key, 2)
    place = jnp.arange(NX, dtype=jnp.float32) / max(NX - 1, 1)
    rising = jnp.exp(jnp.log(3.0) * place)
    channel = jnp.exp(jax.random.uniform(second, (C,), minval=0.0, maxval=jnp.log(4.0)))
    base = jax.random.normal(first, (ZS, C, NX, NY))
    value = base * channel[None, :, None, None] * rising[None, None, :, None]
    return jnp.clip(value, -12.0, 12.0)


def steps_of(own_key, shape, cuts, low, top_value):
    loudness, own = 1.0, jax.random.fold_in(own_key, 6)
    for position, parts in cuts:
        heights = jnp.exp(jax.random.uniform(jax.random.fold_in(own, position), (parts,), jnp.float32, low / len(cuts), top_value / len(cuts)))
        loudness = loudness * jnp.repeat(heights, shape[position] // parts).reshape([-1 if axis == position else 1 for axis in range(len(shape))])
    return loudness


def bell_draw(own_key, shape, scale, bound, cuts=(), kind=jnp.bfloat16):
    drawn = scale * jax.random.normal(own_key, shape, jnp.float32)
    if cuts:
        drawn = drawn * steps_of(own_key, shape, cuts, -0.22, 0.18)
    return jnp.clip(drawn, -bound, bound).astype(kind)


def setup_inputs(seed: int = 0) -> dict:
    streams_of = jax.random.split(jax.random.key(seed), 6)
    features = bell_draw(streams_of[0], (ZS, F, NX, NY), 1.0, 6.0, ((2, 64), (3, 16)))
    head_weight = bell_draw(streams_of[1], (6, F), F ** -0.5, 0.75)
    head_bias = jnp.clip(jax.random.uniform(streams_of[2], (6,), jnp.float32, -1.0, 1.0), -1.0, 1.0)
    probs = jnp.clip(1.0 * jax.random.uniform(streams_of[3], (ZS, C, NX, NY), jnp.float32) ** steps_of(streams_of[3], (ZS, C, NX, NY), ((2, 64), (3, 16)), -0.2, 0.2), 0.0, 1.0)
    cotangent = draw_cotangent(jax.random.fold_in(streams_of[5], 71), 0)
    return dict(features=features, head_weight=head_weight, head_bias=head_bias, probs=probs, cotangent=cotangent)


OFFSETS = ((2, 1), (2, -1), (3, 1), (3, -1), (0, 1), (0, -1))

def shifted(field, dimension, offset):
    length = field.shape[dimension]
    widths = [(1, 1) if axis_dim == dimension else (0, 0) for axis_dim in range(field.ndim)]
    padded = jnp.pad(field, widths)
    return lax.slice_in_dim(padded, 1 + offset, 1 + offset + length, axis=dimension)

def affinities(logits):
    active = jax.nn.sigmoid(logits)
    summed = lax.optimization_barrier(jnp.sum(active, 0))
    coupling = active / (summed + 1.0)
    centre = 1.0 - lax.optimization_barrier(jnp.sum(coupling, 0))
    return (coupling, centre)

def spread(logits, probs):
    coupling, centre = affinities(logits)
    field = probs
    for iteration in range(ITERS):
        result = centre[:, None] * field
        for direction in range(6):
            dimension, offset = OFFSETS[direction]
            result = result + coupling[direction][:, None] * shifted(field, dimension, offset)
        field = result
    return field

def reference(features, head_weight, head_bias, probs, cotangent):
    weight_wide = head_weight.astype(jnp.float32)

    def one_plane(slab_plane):
        return jnp.einsum('kf,fxy->kxy', weight_wide, slab_plane.astype(jnp.float32), precision=lax.Precision.HIGHEST)
    logits = jnp.transpose(lax.map(one_plane, features), (1, 0, 2, 3)) + head_bias[:, None, None, None]
    outcome, pullback = jax.vjp(spread, logits, probs)
    dlogits, grad_probs = pullback(cotangent)
    rounded = jnp.transpose(dlogits.astype(jnp.bfloat16), (1, 0, 2, 3))

    def plane_grad(operands):
        slab_grad, slab_plane = operands
        return jnp.einsum('kxy,fxy->kf', slab_grad.astype(jnp.float32), slab_plane.astype(jnp.float32), precision=lax.Precision.HIGHEST)
    weight_sum = lax.optimization_barrier(jnp.sum(lax.map(plane_grad, (rounded, features)), 0))
    factor = 1.0 / math.sqrt(ZS * NX * NY)
    return (grad_probs, weight_sum * factor, lax.optimization_barrier(jnp.sum(dlogits, (1, 2, 3))) * factor)
```

```python
import math

import jax
import jax.numpy as jnp
from jax import lax
from jax.experimental import pallas as pl
from jax.experimental.pallas import tpu as pltpu
from jax.sharding import PartitionSpec as P

F32 = jnp.float32
BF16 = jnp.bfloat16
MESH = pl.DeviceIdType.MESH
ITERS = 3
FROM_PLUS, FROM_MINUS = 0, 1
H_PART, G_PART = 0, 1


def iota(shape, dim):
    return lax.broadcasted_iota(jnp.int32, shape, dim)


def make_kernel(zs, chans, feats, gx, gy, inner, factor):
    outer = gx // inner
    nx, ny = 8, 128

    def kernel(
        feat_hbm, weight_ref, bias_ref, probs_hbm, cot_hbm,
        out_hbm, gw_ref, gb_ref,
        feat, h_all, g_all, g_out, kap, cen, act, inv, kgrad, dlow, bias_acc, wide,
        send_x, recv_x, send_y, recv_y, sum_a, sum_b, sum_c,
        local_sem, sx_sem, rx_sem, sy_sem, ry_sem, sa_sem, ra_sem, sb_sem, rb_sem, sc_sem, rc_sem,
    ):
        me_x, me_y = lax.axis_index("gx"), lax.axis_index("gy")
        me_in, me_out = lax.rem(me_x, inner), lax.div(me_x, inner)
        right, left = lax.rem(me_x + 1, gx), lax.rem(me_x + gx - 1, gx)
        up, down = lax.rem(me_y + 1, gy), lax.rem(me_y + gy - 1, gy)

        loads = [
            pltpu.make_async_copy(probs_hbm, h_all.at[0, pl.ds(1, zs)], local_sem.at[0]),
            pltpu.make_async_copy(cot_hbm, g_all.at[0, pl.ds(1, zs)], local_sem.at[1]),
            pltpu.make_async_copy(feat_hbm, feat, local_sem.at[2]),
        ]
        for load in loads:
            load.start()

        partners_a = [(me_x, lax.rem(me_y + d, gy)) for d in range(1, gy)]
        partners_b = [(me_out * inner + lax.rem(me_in + d, inner), me_y) for d in range(1, inner)]
        partners_c = [(lax.rem(me_out + d, outer) * inner + me_in, me_y) for d in range(1, outer)]
        greeted = [(left, me_y), (right, me_y)] + partners_a + partners_b + partners_c
        barrier = pltpu.get_barrier_semaphore()
        for partner in greeted:
            pl.semaphore_signal(barrier, inc=1, device_id=partner, device_id_type=MESH)

        blank = jnp.zeros((chans, nx, ny), F32)
        for field in (h_all, g_all):
            for step in range(ITERS):
                field[step, 0] = blank
                field[step, zs + 1] = blank
        kap[0] = jnp.zeros((6, nx, ny), F32)
        kap[zs + 1] = jnp.zeros((6, nx, ny), F32)

        spread = (iota((feats, feats * nx), 1) >> 3) == iota((feats, feats * nx), 0)
        same_x = (iota((6 * nx, feats * nx), 1) & 7) == (iota((6 * nx, feats * nx), 0) & 7)
        weight = weight_ref[...].astype(F32)
        rows = jnp.concatenate(
            [jnp.broadcast_to(weight[k : k + 1, :], (nx, feats)) for k in range(6)], axis=0
        )
        tall = jnp.dot(
            rows.astype(BF16), spread.astype(F32).astype(BF16), preferred_element_type=F32
        )
        wide[...] = jnp.where(same_x, tall, 0.0).astype(BF16)

        row_at = iota((chans, nx, ny), 1)
        lane_at = iota((chans, nx, ny), 2)
        lane = iota((nx, ny), 1)
        has_right, has_left = me_x < gx - 1, me_x > 0
        has_up, has_down = me_y < gy - 1, me_y > 0

        def stage_rows(rnd, part, z, for_right, for_left):
            send_x[rnd, FROM_MINUS, part, z] = jnp.where(has_right, for_right, 0.0)
            send_x[rnd, FROM_PLUS, part, z] = jnp.where(has_left, for_left, 0.0)

        def lanes_of(tile, first, value, source):
            for c in range(chans):
                column = jnp.broadcast_to(value[c][:, source : source + 1], (nx, ny))
                tile = jnp.where(lane == first + c, column, tile)
            return tile

        def stage_lanes(rnd, z, h, p2, p3):
            tile = jnp.zeros((nx, ny), F32)
            ahead = lanes_of(lanes_of(tile, 0, h, ny - 1), chans, p2, ny - 1)
            back = lanes_of(lanes_of(tile, 0, h, 0), chans, p3, 0)
            send_y[rnd, FROM_MINUS, z] = jnp.where(has_up, ahead, 0.0)
            send_y[rnd, FROM_PLUS, z] = jnp.where(has_down, back, 0.0)

        def rim_lanes(rnd, direction, part, z):
            tile = recv_y[rnd, direction, z]
            first = part * chans
            return jnp.stack(
                [jnp.broadcast_to(tile[:, first + c : first + c + 1], (nx, ny)) for c in range(chans)]
            )

        def copies_x(rnd, part):
            return [
                pltpu.make_async_remote_copy(
                    src_ref=send_x.at[rnd, direction, part],
                    dst_ref=recv_x.at[rnd, direction, part],
                    send_sem=sx_sem.at[rnd, direction, part],
                    recv_sem=rx_sem.at[rnd, direction, part],
                    device_id=(target, me_y),
                    device_id_type=MESH,
                )
                for direction, target in ((FROM_MINUS, right), (FROM_PLUS, left))
            ]

        def copies_y(rnd):
            return [
                pltpu.make_async_remote_copy(
                    src_ref=send_y.at[rnd, direction],
                    dst_ref=recv_y.at[rnd, direction],
                    send_sem=sy_sem.at[rnd, direction],
                    recv_sem=ry_sem.at[rnd, direction],
                    device_id=(me_x, target),
                    device_id_type=MESH,
                )
                for direction, target in ((FROM_MINUS, up), (FROM_PLUS, down))
            ]

        def around(rnd, z):
            h = h_all[rnd, z + 1]
            beside = [
                jnp.where(row_at == nx - 1, recv_x[rnd, FROM_PLUS, H_PART, z], pltpu.roll(h, nx - 1, 1)),
                jnp.where(row_at == 0, recv_x[rnd, FROM_MINUS, H_PART, z], pltpu.roll(h, 1, 1)),
                jnp.where(lane_at == ny - 1, rim_lanes(rnd, FROM_PLUS, H_PART, z), pltpu.roll(h, ny - 1, 2)),
                jnp.where(lane_at == 0, rim_lanes(rnd, FROM_MINUS, H_PART, z), pltpu.roll(h, 1, 2)),
                h_all[rnd, z + 2],
                h_all[rnd, z],
            ]
            return h, beside

        def forward(rnd, z):
            h, beside = around(rnd, z)
            result = cen[z] * h
            for k in range(6):
                result = result + kap[z + 1, k] * beside[k]
            return result

        def backward(rnd, z):
            g = g_all[rnd, z + 1]
            p0, p1, p2, p3 = (kap[z + 1, k] * g for k in range(4))
            result = cen[z] * g
            result = result + jnp.where(
                row_at == 0, recv_x[rnd, FROM_MINUS, G_PART, z], pltpu.roll(p0, 1, 1)
            )
            result = result + jnp.where(
                row_at == nx - 1, recv_x[rnd, FROM_PLUS, G_PART, z], pltpu.roll(p1, nx - 1, 1)
            )
            result = result + jnp.where(
                lane_at == 0, rim_lanes(rnd, FROM_MINUS, G_PART, z), pltpu.roll(p2, 1, 2)
            )
            result = result + jnp.where(
                lane_at == ny - 1, rim_lanes(rnd, FROM_PLUS, G_PART, z), pltpu.roll(p3, ny - 1, 2)
            )
            result = result + kap[z, 4] * g_all[rnd, z] + kap[z + 2, 5] * g_all[rnd, z + 2]
            return result

        def stage(rnd, z, h, g):
            k = kap[z + 1]
            stage_rows(rnd, H_PART, z, h[:, nx - 1 :, :], h[:, :1, :])
            stage_rows(
                rnd, G_PART, z,
                k[0][None, nx - 1 :, :] * g[:, nx - 1 :, :], k[1][None, :1, :] * g[:, :1, :],
            )
            stage_lanes(rnd, z, h, k[2] * g, k[3] * g)

        def over_z(body):
            def run(z, carry):
                body(z)
                return carry

            lax.fori_loop(0, zs, run, 0)

        for load in loads:
            load.wait()
        biases = [bias_ref[k] for k in range(6)]

        def head(z):
            logits = jnp.dot(wide[...], feat[z], preferred_element_type=F32)
            active = [jax.nn.sigmoid(logits[k * nx : (k + 1) * nx] + biases[k]) for k in range(6)]
            summed = active[0]
            for k in range(1, 6):
                summed = summed + active[k]
            inverse = 1.0 / (summed + 1.0)
            total = jnp.zeros((nx, ny), F32)
            for k in range(6):
                coupling = active[k] * inverse
                act[z, k] = active[k]
                kap[z + 1, k] = coupling
                total = total + coupling
            inv[z] = inverse
            cen[z] = 1.0 - total
            stage(0, z, h_all[0, z + 1], g_all[0, z + 1])

        over_z(head)
        pl.semaphore_wait(barrier, len(greeted))

        pending = []

        def launch(rnd):
            copies = copies_y(rnd) + copies_x(rnd, H_PART) + copies_x(rnd, G_PART)
            for copy in copies:
                copy.start()
            pending.extend(copies)
            return copies

        for rnd in range(ITERS - 1):
            for copy in launch(rnd):
                copy.wait_recv()

            def advance(z, rnd=rnd):
                h, g = forward(rnd, z), backward(rnd, z)
                h_all[rnd + 1, z + 1] = h
                g_all[rnd + 1, z + 1] = g
                stage(rnd + 1, z, h, g)

            over_z(advance)
        last = launch(ITERS - 1)

        def terms(z, rounds):
            parts = [jnp.zeros((nx, ny), F32) for _ in range(7)]
            for rnd in rounds:
                g = g_all[ITERS - 1 - rnd, z + 1]
                h, beside = around(rnd, z)
                for k in range(6):
                    parts[k] = parts[k] + jnp.sum(g * beside[k], 0)
                parts[6] = parts[6] + jnp.sum(g * h, 0)
            return parts

        def early(z):
            parts = terms(z, range(ITERS - 1))
            for k in range(7):
                kgrad[z, k] = parts[k]

        over_z(early)
        bias_acc[...] = jnp.zeros((6, nx, ny), F32)
        for copy in last:
            copy.wait_recv()

        def late(z):
            parts = terms(z, [ITERS - 1])
            inner_sum = jnp.zeros((nx, ny), F32)
            effective = []
            centre_grad = parts[6] + kgrad[z, 6]
            for k in range(6):
                value = parts[k] + kgrad[z, k] - centre_grad
                effective.append(value)
                inner_sum = inner_sum + value * kap[z + 1, k]
            pieces = []
            for k in range(6):
                active = act[z, k]
                slope = (effective[k] - inner_sum) * inv[z] * active * (1.0 - active)
                bias_acc[k] += slope
                pieces.append(slope)
            dlow[z] = jnp.concatenate(pieces, axis=0).astype(BF16)

        over_z(late)

        total = jnp.zeros((6 * nx, feats * nx), F32)
        for z in range(0, zs, 2):
            total = total + lax.dot_general(
                jnp.concatenate([dlow[z], dlow[z + 1]], axis=1),
                jnp.concatenate([feat[z], feat[z + 1]], axis=1),
                (((1,), (1,)), ((), ())),
                preferred_element_type=F32,
            )
        total = jnp.where(same_x, total, 0.0)
        by_k = jnp.concatenate(
            [jnp.sum(total[k * nx : (k + 1) * nx], 0, keepdims=True) for k in range(6)]
            + [jnp.zeros((2, feats * nx), F32)],
            axis=0,
        )
        fold = ((iota((feats * nx, 2 * feats), 0) >> 3) == iota((feats * nx, 2 * feats), 1)).astype(F32)
        by_f = jnp.dot(by_k, fold, precision=lax.Precision.HIGHEST, preferred_element_type=F32)
        lane_row = iota((1, ny), 1)
        payload = [
            jnp.where(
                lane_row < feats,
                by_f[2 * r : 2 * r + 1],
                pltpu.roll(by_f[2 * r + 1 : 2 * r + 2], feats, 1),
            )
            for r in range(3)
        ]
        bias_row = jnp.zeros((1, ny), F32)
        for k in range(6):
            amount = jnp.sum(jnp.sum(bias_acc[k], 0, keepdims=True), 1, keepdims=True)
            bias_row = jnp.where(lane_row == k, amount, bias_row)
        payload = jnp.concatenate(payload + [bias_row], axis=0)

        def exchange(buffer, me, partners, positions, send_sem, recv_sem, value):
            buffer[me] = value
            copies = []
            for d, (partner, position) in enumerate(zip(partners, positions)):
                copy = pltpu.make_async_remote_copy(
                    src_ref=buffer.at[me],
                    dst_ref=buffer.at[me],
                    send_sem=send_sem.at[d],
                    recv_sem=recv_sem.at[d],
                    device_id=partner,
                    device_id_type=MESH,
                )
                copy.start()
                copies.append(copy)
            pending.extend(copies)
            return copies

        def gather(buffer, copies, count):
            for copy in copies:
                copy.wait_recv()
            value = buffer[0]
            for i in range(1, count):
                value = value + buffer[i]
            return value

        first = exchange(sum_a, me_y, partners_a, partners_a, sa_sem, ra_sem, payload)

        def finish(z):
            g_out[z] = backward(ITERS - 1, z)

        over_z(finish)
        store = pltpu.make_async_copy(g_out, out_hbm, local_sem.at[3])
        store.start()

        value = gather(sum_a, first, gy)
        second = exchange(sum_b, me_in, partners_b, partners_b, sb_sem, rb_sem, value)
        value = gather(sum_b, second, inner)
        third = exchange(sum_c, me_out, partners_c, partners_c, sc_sem, rc_sem, value)
        value = gather(sum_c, third, outer) * factor
        for k in range(6):
            row = value[k // 2 : k // 2 + 1]
            if k % 2:
                row = pltpu.roll(row, feats, 1)
            gw_ref[k : k + 1, :] = row[:, :feats]
        gb_ref[...] = value[3:4, :6]
        for copy in pending:
            copy.wait_send()
        store.wait()

    return kernel


def inner_of(gx):
    return 8 if gx == 64 else 2


def per_device(features, head_weight, head_bias, probs, cotangent):
    zs, feats, nx, ny = features.shape
    chans = probs.shape[1]
    gx, gy = lax.axis_size("gx"), lax.axis_size("gy")
    inner = inner_of(gx)
    outer = gx // inner
    factor = 1.0 / math.sqrt(zs * nx * ny * gx * gy)
    field = (zs + 2, chans, nx, ny)
    dma = pltpu.SemaphoreType.DMA
    rim_x = (ITERS, 2, 2, zs, chans, 1, ny)
    rim_y = (ITERS, 2, zs, nx, ny)
    hbm = pl.BlockSpec(memory_space=pltpu.HBM)
    vmem = pl.BlockSpec(memory_space=pltpu.VMEM)
    grad_probs, grad_weight, grad_bias = pl.pallas_call(
        make_kernel(zs, chans, feats, gx, gy, inner, factor),
        out_shape=(
            jax.ShapeDtypeStruct(probs.shape, F32),
            jax.ShapeDtypeStruct((6, feats), F32),
            jax.ShapeDtypeStruct((1, 6), F32),
        ),
        in_specs=[hbm, vmem, pl.BlockSpec(memory_space=pltpu.SMEM), hbm, hbm],
        out_specs=(hbm, vmem, vmem),
        scratch_shapes=[
            pltpu.VMEM((zs, feats * nx, ny), BF16),
            pltpu.VMEM((ITERS,) + field, F32),
            pltpu.VMEM((ITERS,) + field, F32),
            pltpu.VMEM((zs, chans, nx, ny), F32),
            pltpu.VMEM((zs + 2, 6, nx, ny), F32),
            pltpu.VMEM((zs, nx, ny), F32),
            pltpu.VMEM((zs, 6, nx, ny), F32),
            pltpu.VMEM((zs, nx, ny), F32),
            pltpu.VMEM((zs, 7, nx, ny), F32),
            pltpu.VMEM((zs, 6 * nx, ny), BF16),
            pltpu.VMEM((6, nx, ny), F32),
            pltpu.VMEM((6 * nx, feats * nx), BF16),
            pltpu.VMEM(rim_x, F32),
            pltpu.VMEM(rim_x, F32),
            pltpu.VMEM(rim_y, F32),
            pltpu.VMEM(rim_y, F32),
            pltpu.VMEM((gy, 4, ny), F32),
            pltpu.VMEM((inner, 4, ny), F32),
            pltpu.VMEM((outer, 4, ny), F32),
            dma((4,)),
            dma((ITERS, 2, 2)),
            dma((ITERS, 2, 2)),
            dma((ITERS, 2)),
            dma((ITERS, 2)),
            dma((gy - 1,)),
            dma((gy - 1,)),
            dma((inner - 1,)),
            dma((inner - 1,)),
            dma((outer - 1,)),
            dma((outer - 1,)),
        ],
        compiler_params=pltpu.CompilerParams(
            collective_id=0, has_side_effects=True, vmem_limit_bytes=63 * 1024 * 1024
        ),
        name="spread_backward",
    )(features.reshape(zs, feats * nx, ny), head_weight, head_bias, probs, cotangent)
    return grad_probs, grad_weight, grad_bias.reshape(6)


def solution(mesh):
    spec = P(None, None, "gx", "gy")
    return jax.shard_map(
        per_device,
        mesh=mesh,
        in_specs=(spec, P(), P(), spec, spec),
        out_specs=(spec, P(), P()),
        check_vma=False,
    )
```

```python
import math

import jax
import jax.numpy as jnp
from jax import lax
from jax.experimental import pallas as pl
from jax.experimental.pallas import tpu as pltpu
from jax.sharding import PartitionSpec as P

F32 = jnp.float32
BF16 = jnp.bfloat16
MESH = pl.DeviceIdType.MESH
ITERS = 3
NX, NY = 8, 128
RING = 16
EDGE = 16
LOW, HIGH = 3, 12
SIDES = [(dx, dy) for dx in (1, -1, 0) for dy in (0, 1, -1) if dx or dy]


def iota(shape, dim):
    return lax.broadcasted_iota(jnp.int32, shape, dim)


def rows_of(dx):
    if dx == 0:
        return pl.ds(0, NX), pl.ds(0, NX)
    if dx > 0:
        return pl.ds(NX - 3, 3), pl.ds(RING - 3, 3)
    return pl.ds(0, 3), pl.ds(NX, 3)


def make_kernel(zs, chans, feats, gx, gy, inner, factor):
    outer = gx // inner
    inside = pl.ds(1, zs)

    def kernel(
        feat_hbm, weight_ref, bias_ref, probs_hbm, cot_hbm,
        out_hbm, sum_ref,
        feat, hs, gs, g_out, kap, kst, act, inv, dlow, bias_acc, wide, expand,
        sf, sk, flat, sum_a, sum_b, sum_c,
        local_sem, row_send, row_recv, strip_send, strip_recv,
        sa_sem, ra_sem, sb_sem, rb_sem, sc_sem, rc_sem,
    ):
        me_x, me_y = lax.axis_index("gx"), lax.axis_index("gy")
        me_in, me_out = lax.rem(me_x, inner), lax.div(me_x, inner)

        def at(dx, dy):
            return lax.rem(me_x + dx + gx, gx), lax.rem(me_y + dy + gy, gy)

        partners_a = [(me_x, lax.rem(me_y + d, gy)) for d in range(1, gy)]
        partners_b = [(me_out * inner + lax.rem(me_in + d, inner), me_y) for d in range(1, inner)]
        partners_c = [(lax.rem(me_out + d, outer) * inner + me_in, me_y) for d in range(1, outer)]
        greeted = [at(dx, dy) for dx, dy in SIDES if dx] + partners_a + partners_b + partners_c
        barrier = pltpu.get_barrier_semaphore()
        for partner in greeted:
            pl.semaphore_signal(barrier, inc=1, device_id=partner, device_id_type=MESH)

        fields_in = [
            pltpu.make_async_copy(source, field.at[0, inside, pl.ds(0, chans), pl.ds(0, NX)], local_sem.at[i])
            for i, (source, field) in enumerate(((probs_hbm, hs), (cot_hbm, gs)))
        ]
        feats_in = [
            pltpu.make_async_copy(feat_hbm.at[z], feat.at[z], local_sem.at[2 + z]) for z in range(zs)
        ]
        for load in fields_in + feats_in:
            load.start()

        for field in (hs, gs):
            for step in range(ITERS):
                for z in (0, zs + 1):
                    field[step, z] = jnp.zeros((chans + 1, RING, NY), F32)
        for coefs in (kap, kst):
            for z in (0, zs + 1):
                coefs[z] = jnp.zeros((7, RING, NY), F32)

        spread = (iota((feats, feats * NX), 1) >> 3) == iota((feats, feats * NX), 0)
        same_x = (iota((6 * NX, feats * NX), 1) & 7) == (iota((6 * NX, feats * NX), 0) & 7)
        weight = weight_ref[...].astype(F32)
        rows = jnp.concatenate(
            [jnp.broadcast_to(weight[k : k + 1, :], (NX, feats)) for k in range(6)], axis=0
        )
        tall = jnp.dot(
            rows.astype(BF16), spread.astype(F32).astype(BF16), preferred_element_type=F32
        )
        wide[...] = jnp.where(same_x, tall, 0.0).astype(BF16)
        here, there = iota((NY, 6 * NY), 0), iota((NY, 6 * NY), 1)
        expand[...] = (((here >> 4) == (there >> 7)) & ((here & 15) == (there & 15))).astype(F32)

        lane = iota((NX, NY), 1)
        lane_j = lane & (EDGE - 1)
        ring_lane = iota((RING, NY), 1)
        ring_j = ring_lane & (EDGE - 1)
        ring_row = iota((RING, NY), 0)
        has_right, has_left = me_x < gx - 1, me_x > 0
        has_up, has_down = me_y < gy - 1, me_y > 0

        def packed(values):
            tile = jnp.zeros((NX, NY), F32)
            for i, value in enumerate(values):
                tile = jnp.where((lane >> 4) == i, pltpu.roll(value, i * EDGE + 4, 1), tile)
            return jnp.where(lane_j < 8, tile, 0.0)

        def unpacked(own, low, high):
            seen = (
                (ring_row < NX) | ((ring_row < NX + 4) & has_right) | ((ring_row >= NX + 4) & has_left)
            )
            low = jnp.where(has_down, low, 0.0)
            high = jnp.where(has_up, high, 0.0)
            near = jnp.where(ring_j < 4, low, own)
            far = pltpu.roll(jnp.where(ring_j < 4, own, high), 8, 1)
            return jnp.where(seen, jnp.where(ring_j < 8, near, far), 0.0)

        def over_z(body):
            def run(z, carry):
                body(z)
                return carry

            lax.fori_loop(0, zs, run, 0, unroll=True)

        def remote(source, target, send_sem, recv_sem, device):
            return pltpu.make_async_remote_copy(
                src_ref=source, dst_ref=target, send_sem=send_sem, recv_sem=recv_sem,
                device_id=device, device_id_type=MESH,
            )

        pending, arriving = [], []

        def send(copies):
            for copy in copies:
                copy.start()
            pending.extend(copies)
            arriving.extend(copies)

        def row_copies(which, view):
            return [
                remote(
                    view(rows_of(dx)[0]), view(rows_of(dx)[1]),
                    row_send.at[which, i], row_recv.at[which, i], at(dx, 0),
                )
                for i, dx in enumerate((1, -1))
            ]

        def strip_copies(which, view):
            return [
                remote(
                    view(0, rows_of(dx)[0]), view((0, 1, 2)[dy], rows_of(dx)[1]),
                    strip_send.at[which, i], strip_recv.at[which, i], at(dx, dy),
                )
                for i, (dx, dy) in enumerate(SIDES)
            ]

        for load in fields_in:
            load.wait()

        def pack_fields(z):
            sf[0, 0, z, :NX] = packed([hs[0, z + 1, c, :NX] for c in range(chans)])
            sf[0, 1, z, :NX] = packed([gs[0, z + 1, c, :NX] for c in range(chans)])

        over_z(pack_fields)
        pl.semaphore_wait(barrier, len(greeted))
        send(row_copies(0, lambda r: hs.at[0, inside, pl.ds(0, chans), r]))
        send(row_copies(1, lambda r: gs.at[0, inside, pl.ds(0, chans), r]))
        send(strip_copies(0, lambda column, r: sf.at[column, pl.ds(0, 2), pl.ds(0, zs), r]))

        biases = [bias_ref[k] for k in range(6)]
        for load in feats_in:
            load.wait()

        def head(z):
            logits = jnp.dot(wide[...], feat[z], preferred_element_type=F32)
            active = [jax.nn.sigmoid(logits[k * NX : (k + 1) * NX] + biases[k]) for k in range(6)]
            summed = active[0]
            for k in range(1, 6):
                summed = summed + active[k]
            inverse = 1.0 / (summed + 1.0)
            coupling = [active[k] * inverse for k in range(6)]
            for k in range(6):
                act[z, k] = active[k]
                kap[z + 1, k, :NX] = coupling[k]
            inv[z] = inverse
            sk[0, z, :NX] = packed(coupling)

        over_z(head)
        send(row_copies(2, lambda r: kap.at[inside, pl.ds(0, 6), r]))
        send(strip_copies(1, lambda column, r: sk.at[column, pl.ds(0, zs), r]))
        for copy in arriving:
            copy.wait_recv()

        def clear(rows):
            hs[0, 1 : zs + 1, :chans, rows] = jnp.zeros((zs, chans, 4, NY), F32)
            kap[1 : zs + 1, :6, rows] = jnp.zeros((zs, 6, 4, NY), F32)

        @pl.when(me_x == gx - 1)
        def _():
            clear(slice(NX, NX + 4))

        @pl.when(me_x == 0)
        def _():
            clear(slice(NX + 4, RING))

        def assemble(z):
            hs[0, z + 1, chans] = unpacked(sf[0, 0, z], sf[1, 0, z], sf[2, 0, z])
            gs[0, z + 1, chans] = unpacked(sf[0, 1, z], sf[1, 1, z], sf[2, 1, z])
            flat[pl.ds(z * RING, RING)] = unpacked(sk[0, z], sk[1, z], sk[2, z])

        over_z(assemble)
        strips = jnp.dot(
            flat[...], expand[...], precision=lax.Precision.HIGHEST, preferred_element_type=F32
        )
        for z in range(zs):
            for coefs, value in (
                (kst, [strips[z * RING : (z + 1) * RING, k * NY : (k + 1) * NY] for k in range(6)]),
                (kap, [kap[z + 1, k] for k in range(6)]),
            ):
                centre = 1.0
                for k in range(6):
                    centre = centre - value[k]
                    if coefs is kst:
                        coefs[z + 1, k] = value[k]
                coefs[z + 1, 6] = centre

        def columns(strip, j):
            return jnp.stack(
                [
                    jnp.broadcast_to(strip[:, c * EDGE + j : c * EDGE + j + 1], strip.shape)
                    for c in range(chans)
                ]
            )

        def around(rnd, z, rows):
            h, strip = hs[rnd, z + 1, :chans], hs[rnd, z + 1, chans, :rows]
            shape = (chans, rows, NY)
            lanes = iota(shape, 2)
            centre = h[:, :rows]
            return centre, [
                pltpu.roll(h, RING - 1, 1)[:, :rows],
                pltpu.roll(h, 1, 1)[:, :rows],
                jnp.where(lanes == NY - 1, columns(strip, HIGH), pltpu.roll(centre, NY - 1, 2)),
                jnp.where(lanes == 0, columns(strip, LOW), pltpu.roll(centre, 1, 2)),
                hs[rnd, z + 2, :chans, :rows],
                hs[rnd, z, :chans, :rows],
            ]

        def forward(rnd, z):
            h, beside = around(rnd, z, RING)
            result = kap[z + 1, 6] * h
            for k in range(6):
                result = result + kap[z + 1, k] * beside[k]
            strip = hs[rnd, z + 1, chans]
            edge = kst[z + 1, 6] * strip
            for k, value in enumerate((
                pltpu.roll(strip, RING - 1, 0),
                pltpu.roll(strip, 1, 0),
                pltpu.roll(strip, NY - 1, 1),
                pltpu.roll(strip, 1, 1),
                hs[rnd, z + 2, chans],
                hs[rnd, z, chans],
            )):
                edge = edge + kst[z + 1, k] * value
            hs[rnd + 1, z + 1, :chans] = result
            hs[rnd + 1, z + 1, chans] = edge

        def backward(rnd, z, rows):
            g, strip = gs[rnd, z + 1, :chans], gs[rnd, z + 1, chans]
            lanes = iota((chans, rows, NY), 2)
            near = g[:, :rows]
            edge = [kst[z + 1, k] * strip for k in range(4)]
            result = kap[z + 1, 6, :rows] * near
            result = result + pltpu.roll(kap[z + 1, 0] * g, 1, 1)[:, :rows]
            result = result + pltpu.roll(kap[z + 1, 1] * g, RING - 1, 1)[:, :rows]
            result = result + jnp.where(
                lanes == 0,
                columns(edge[2][:rows], LOW),
                pltpu.roll(kap[z + 1, 2, :rows] * near, 1, 2),
            )
            result = result + jnp.where(
                lanes == NY - 1,
                columns(edge[3][:rows], HIGH),
                pltpu.roll(kap[z + 1, 3, :rows] * near, NY - 1, 2),
            )
            result = result + kap[z, 4, :rows] * gs[rnd, z, :chans, :rows]
            result = result + kap[z + 2, 5, :rows] * gs[rnd, z + 2, :chans, :rows]
            if rows == NX:
                return result
            strip = kst[z + 1, 6] * strip
            strip = strip + pltpu.roll(edge[0], 1, 0) + pltpu.roll(edge[1], RING - 1, 0)
            strip = strip + pltpu.roll(edge[2], 1, 1) + pltpu.roll(edge[3], NY - 1, 1)
            strip = strip + kst[z, 4] * gs[rnd, z, chans] + kst[z + 2, 5] * gs[rnd, z + 2, chans]
            gs[rnd + 1, z + 1, :chans] = result
            gs[rnd + 1, z + 1, chans] = strip

        for rnd in range(ITERS - 1):

            def advance(z, rnd=rnd):
                forward(rnd, z)
                backward(rnd, z, RING)

            over_z(advance)

        bias_acc[...] = jnp.zeros((6, NX, NY), F32)

        def slopes(z):
            parts = [jnp.zeros((NX, NY), F32) for _ in range(7)]
            for rnd in range(ITERS):
                g = gs[ITERS - 1 - rnd, z + 1, :chans, :NX]
                h, beside = around(rnd, z, NX)
                for k in range(6):
                    parts[k] = parts[k] + jnp.sum(g * beside[k], 0)
                parts[6] = parts[6] + jnp.sum(g * h, 0)
            inner_sum = jnp.zeros((NX, NY), F32)
            effective = []
            for k in range(6):
                value = parts[k] - parts[6]
                effective.append(value)
                inner_sum = inner_sum + value * kap[z + 1, k, :NX]
            pieces = []
            for k in range(6):
                active = act[z, k]
                slope = (effective[k] - inner_sum) * inv[z] * active * (1.0 - active)
                bias_acc[k] += slope
                pieces.append(slope)
            dlow[z] = jnp.concatenate(pieces, axis=0).astype(BF16)

        over_z(slopes)

        total = jnp.zeros((6 * NX, feats * NX), F32)
        for z in range(0, zs, 2):
            total = total + lax.dot_general(
                jnp.concatenate([dlow[z], dlow[z + 1]], axis=1),
                jnp.concatenate([feat[z], feat[z + 1]], axis=1),
                (((1,), (1,)), ((), ())),
                preferred_element_type=F32,
            )
        total = jnp.where(same_x, total, 0.0)
        by_k = jnp.concatenate(
            [jnp.sum(total[k * NX : (k + 1) * NX], 0, keepdims=True) for k in range(6)]
            + [jnp.zeros((2, feats * NX), F32)],
            axis=0,
        )
        fold = ((iota((feats * NX, 2 * feats), 0) >> 3) == iota((feats * NX, 2 * feats), 1)).astype(F32)
        by_f = jnp.dot(by_k, fold, precision=lax.Precision.HIGHEST, preferred_element_type=F32)
        lane_row = iota((1, NY), 1)
        payload = [
            jnp.where(
                lane_row < feats,
                by_f[2 * r : 2 * r + 1],
                pltpu.roll(by_f[2 * r + 1 : 2 * r + 2], feats, 1),
            )
            for r in range(3)
        ]
        bias_row = jnp.zeros((1, NY), F32)
        for k in range(6):
            amount = jnp.sum(jnp.sum(bias_acc[k], 0, keepdims=True), 1, keepdims=True)
            bias_row = jnp.where(lane_row == k, amount, bias_row)
        payload = jnp.concatenate(payload + [bias_row], axis=0)

        def exchange(buffer, me, partners, send_sem, recv_sem, value):
            buffer[me] = value
            copies = [
                remote(buffer.at[me], buffer.at[me], send_sem.at[d], recv_sem.at[d], partner)
                for d, partner in enumerate(partners)
            ]
            for copy in copies:
                copy.start()
            pending.extend(copies)
            return copies

        def gather(buffer, copies, count):
            for copy in copies:
                copy.wait_recv()
            value = buffer[0]
            for i in range(1, count):
                value = value + buffer[i]
            return value

        first = exchange(sum_a, me_y, partners_a, sa_sem, ra_sem, payload)

        def finish(z):
            g_out[z] = backward(ITERS - 1, z, NX)

        over_z(finish)
        store = pltpu.make_async_copy(g_out, out_hbm, local_sem.at[2 + zs])
        store.start()

        value = gather(sum_a, first, gy)
        second = exchange(sum_b, me_in, partners_b, sb_sem, rb_sem, value)
        value = gather(sum_b, second, inner)
        third = exchange(sum_c, me_out, partners_c, sc_sem, rc_sem, value)
        sum_ref[...] = gather(sum_c, third, outer) * factor
        for copy in pending:
            copy.wait_send()
        store.wait()

    return kernel


def deliver(feats):
    def kernel(field, sums, grad_probs, grad_weight, grad_bias, sems):
        copies = [
            pltpu.make_async_copy(field.at[z], grad_probs.at[z], sems.at[z])
            for z in range(field.shape[0])
        ]
        for copy in copies:
            copy.start()
        for k in range(6):
            row = sums[k // 2 : k // 2 + 1, :]
            if k % 2:
                row = pltpu.roll(row, feats, 1)
            grad_weight[k : k + 1, :] = row[:, :feats]
        grad_bias[...] = sums[3:4, :6]
        for copy in copies:
            copy.wait()

    return kernel


def inner_of(gx):
    return 8 if gx == 64 else 2


def per_device(features, head_weight, head_bias, probs, cotangent):
    zs, feats, nx, ny = features.shape
    chans = probs.shape[1]
    gx, gy = lax.axis_size("gx"), lax.axis_size("gy")
    inner = inner_of(gx)
    outer = gx // inner
    factor = 1.0 / math.sqrt(zs * nx * ny * gx * gy)
    dma = pltpu.SemaphoreType.DMA
    hbm = pl.BlockSpec(memory_space=pltpu.HBM)
    vmem = pl.BlockSpec(memory_space=pltpu.VMEM)
    field = pltpu.VMEM((ITERS, zs + 2, chans + 1, RING, ny), F32)
    coefs = pltpu.VMEM((zs + 2, 7, RING, ny), F32)
    grad_field, sums = pl.pallas_call(
        make_kernel(zs, chans, feats, gx, gy, inner, factor),
        out_shape=(
            jax.ShapeDtypeStruct(probs.shape, F32),
            jax.ShapeDtypeStruct((4, ny), F32),
        ),
        in_specs=[hbm, vmem, pl.BlockSpec(memory_space=pltpu.SMEM), hbm, hbm],
        out_specs=(hbm, vmem),
        scratch_shapes=[
            pltpu.VMEM((zs, feats * nx, ny), BF16),
            field,
            field,
            pltpu.VMEM((zs, chans, nx, ny), F32),
            coefs,
            coefs,
            pltpu.VMEM((zs, 6, nx, ny), F32),
            pltpu.VMEM((zs, nx, ny), F32),
            pltpu.VMEM((zs, 6 * nx, ny), BF16),
            pltpu.VMEM((6, nx, ny), F32),
            pltpu.VMEM((6 * nx, feats * nx), BF16),
            pltpu.VMEM((ny, 6 * ny), F32),
            pltpu.VMEM((3, 2, zs, RING, ny), F32),
            pltpu.VMEM((3, zs, RING, ny), F32),
            pltpu.VMEM((zs * RING, ny), F32),
            pltpu.VMEM((gy, 4, ny), F32),
            pltpu.VMEM((inner, 4, ny), F32),
            pltpu.VMEM((outer, 4, ny), F32),
            dma((3 + zs,)),
            dma((3, 2)),
            dma((3, 2)),
            dma((2, len(SIDES))),
            dma((2, len(SIDES))),
            dma((gy - 1,)),
            dma((gy - 1,)),
            dma((inner - 1,)),
            dma((inner - 1,)),
            dma((outer - 1,)),
            dma((outer - 1,)),
        ],
        compiler_params=pltpu.CompilerParams(
            collective_id=0, has_side_effects=True, vmem_limit_bytes=63 * 1024 * 1024
        ),
        name="spread_backward",
    )(features.reshape(zs, feats * nx, ny), head_weight, head_bias, probs, cotangent)
    grad_probs, grad_weight, grad_bias = pl.pallas_call(
        deliver(feats),
        out_shape=(
            jax.ShapeDtypeStruct(probs.shape, F32),
            jax.ShapeDtypeStruct((6, feats), F32),
            jax.ShapeDtypeStruct((1, 6), F32),
        ),
        in_specs=[pl.BlockSpec(memory_space=pl.ANY), vmem],
        out_specs=(hbm, vmem, vmem),
        scratch_shapes=[dma((zs,))],
        name="deliver",
    )(grad_field, sums)
    return grad_probs, grad_weight, grad_bias.reshape(6)


def solution(mesh):
    spec = P(None, None, "gx", "gy")
    return jax.shard_map(
        per_device,
        mesh=mesh,
        in_specs=(spec, P(), P(), spec, spec),
        out_specs=(spec, P(), P()),
        check_vma=False,
    )
```

```python
import math

import jax
import jax.numpy as jnp
from jax import lax
from jax.experimental import pallas as pl
from jax.experimental.pallas import tpu as pltpu
from jax.sharding import PartitionSpec as P

F32 = jnp.float32
BF16 = jnp.bfloat16
MESH = pl.DeviceIdType.MESH
ITERS = 3
NX, NY = 8, 128
RING = 16
EDGE = 16
LOW, HIGH = 3, 12
SIDES = [(dx, dy) for dx in (1, -1, 0) for dy in (0, 1, -1) if dx or dy]


def iota(shape, dim):
    return lax.broadcasted_iota(jnp.int32, shape, dim)


def rows_of(dx, count):
    if dx == 0:
        return pl.ds(0, NX), pl.ds(0, NX)
    if dx > 0:
        return pl.ds(NX - count, count), pl.ds(RING - count, count)
    return pl.ds(0, count), pl.ds(NX, count)


def make_kernel(zs, chans, feats, gx, gy, inner, factor):
    outer = gx // inner
    inside = pl.ds(1, zs)

    def kernel(
        feat_hbm, weight_ref, bias_ref, probs_hbm, cot_hbm,
        out_hbm, sum_ref,
        feat, hs, gs, g_out, kap, kst, act, inv, dlow, bias_acc, wide, expand,
        sf, sk, flat, far_g, far_k, sum_a, sum_b, sum_c,
        local_sem, row_send, row_recv, strip_send, strip_recv,
        sa_sem, ra_sem, sb_sem, rb_sem, sc_sem, rc_sem,
    ):
        me_x, me_y = lax.axis_index("gx"), lax.axis_index("gy")
        me_in, me_out = lax.rem(me_x, inner), lax.div(me_x, inner)

        def at(dx, dy):
            return lax.rem(me_x + dx + gx, gx), lax.rem(me_y + dy + gy, gy)

        partners_a = [(me_x, lax.rem(me_y + d, gy)) for d in range(1, gy)]
        partners_b = [(me_out * inner + lax.rem(me_in + d, inner), me_y) for d in range(1, inner)]
        partners_c = [(lax.rem(me_out + d, outer) * inner + me_in, me_y) for d in range(1, outer)]
        greeted = [at(dx, dy) for dx, dy in SIDES if dx] + partners_a + partners_b + partners_c
        fields_in = [
            pltpu.make_async_copy(source, field.at[0, inside, pl.ds(0, chans), pl.ds(0, NX)], local_sem.at[i])
            for i, (source, field) in enumerate(((probs_hbm, hs), (cot_hbm, gs)))
        ]
        feats_in = [
            pltpu.make_async_copy(feat_hbm.at[z], feat.at[z], local_sem.at[2 + z]) for z in range(zs)
        ]
        for load in fields_in:
            load.start()
        barrier = pltpu.get_barrier_semaphore()
        for partner in greeted:
            pl.semaphore_signal(barrier, inc=1, device_id=partner, device_id_type=MESH)
        for load in feats_in:
            load.start()

        for field in (hs, gs):
            for step in range(ITERS):
                for z in (0, zs + 1):
                    field[step, z] = jnp.zeros((chans + 1, RING, NY), F32)
        for coefs in (kap, kst):
            for z in (0, zs + 1):
                coefs[z] = jnp.zeros((7, RING, NY), F32)

        spread = (iota((feats, feats * NX), 1) >> 3) == iota((feats, feats * NX), 0)
        same_x = (iota((6 * NX, feats * NX), 1) & 7) == (iota((6 * NX, feats * NX), 0) & 7)
        weight = weight_ref[...].astype(F32)
        rows = jnp.concatenate(
            [jnp.broadcast_to(weight[k : k + 1, :], (NX, feats)) for k in range(6)], axis=0
        )
        tall = jnp.dot(
            rows.astype(BF16), spread.astype(F32).astype(BF16), preferred_element_type=F32
        )
        wide[...] = jnp.where(same_x, tall, 0.0).astype(BF16)
        here, there = iota((NY, 6 * NY), 0), iota((NY, 6 * NY), 1)
        expand[...] = (((here >> 4) == (there >> 7)) & ((here & 15) == (there & 15))).astype(F32)

        lane = iota((NX, NY), 1)
        lane_j = lane & (EDGE - 1)
        ring_lane = iota((RING, NY), 1)
        ring_j = ring_lane & (EDGE - 1)
        ring_row = iota((RING, NY), 0)
        has_right, has_left = me_x < gx - 1, me_x > 0
        has_up, has_down = me_y < gy - 1, me_y > 0

        def packed(values):
            tile = jnp.zeros((NX, NY), F32)
            for i, value in enumerate(values):
                tile = jnp.where((lane >> 4) == i, pltpu.roll(value, i * EDGE + 4, 1), tile)
            return jnp.where(lane_j < 8, tile, 0.0)

        def unpacked(own, low, high, first):
            seen = (
                (ring_row < NX) | ((ring_row < NX + 4) & has_right) | ((ring_row >= NX + 4) & has_left)
            )
            low = jnp.where(has_down, low, 0.0)
            high = jnp.where(has_up, high, 0.0)
            near = jnp.where(ring_j < first + 4, low, own)
            far = jnp.where(ring_j < first + 4, own, high)
            if first:
                near = pltpu.roll(near, NY - first, 1)
            else:
                far = pltpu.roll(far, 8, 1)
            return jnp.where(seen, jnp.where(ring_j < 8, near, far), 0.0)

        def over_z(body):
            def run(z, carry):
                body(z)
                return carry

            lax.fori_loop(0, zs, run, 0, unroll=True)

        def remote(source, target, send_sem, recv_sem, device):
            return pltpu.make_async_remote_copy(
                src_ref=source, dst_ref=target, send_sem=send_sem, recv_sem=recv_sem,
                device_id=device, device_id_type=MESH,
            )

        pending, arriving = [], []

        def send(copies, awaited=True):
            for copy in copies:
                copy.start()
            pending.extend(copies)
            if awaited:
                arriving.extend(copies)
            return copies

        def row_copies(which, count, view):
            return [
                remote(
                    view(rows_of(dx, count)[0]), view(rows_of(dx, count)[1]),
                    row_send.at[which, i], row_recv.at[which, i], at(dx, 0),
                )
                for i, dx in enumerate((1, -1))
            ]

        def far_copies(which, view, target):
            return [
                remote(
                    view(pl.ds(row, 1)), target.at[i, pl.ds(0, zs), pl.ds(0, target.shape[2]), pl.ds(0, 1)],
                    row_send.at[which, i], row_recv.at[which, i], at(dx, 0),
                )
                for i, (dx, row) in enumerate(((1, NX - 3), (-1, 2)))
            ]

        def strip_copies(which, strip):
            return [
                remote(
                    strip.at[0, pl.ds(0, zs), rows_of(dx, 3)[0]],
                    strip.at[(0, 1, 2)[dy], pl.ds(0, zs), rows_of(dx, 3)[1]],
                    strip_send.at[which, i], strip_recv.at[which, i], at(dx, dy),
                )
                for i, (dx, dy) in enumerate(SIDES)
            ]

        for load in fields_in:
            load.wait()

        def pack_fields(z):
            of_h = packed([hs[0, z + 1, c, :NX] for c in range(chans)])
            of_g = packed([gs[0, z + 1, c, :NX] for c in range(chans)])
            sf[0, z, :NX] = of_h + pltpu.roll(of_g, 8, 1)

        over_z(pack_fields)
        pl.semaphore_wait(barrier, len(greeted))
        g_rows = lambda r: gs.at[0, inside, pl.ds(0, chans), r]
        k_rows = lambda r: kap.at[inside, pl.ds(0, 6), r]
        send(row_copies(0, 3, lambda r: hs.at[0, inside, pl.ds(0, chans), r]))
        send(row_copies(1, 2, g_rows))
        send(strip_copies(0, sf))

        biases = [bias_ref[k] for k in range(6)]
        for load in feats_in:
            load.wait()

        def head(z):
            logits = jnp.dot(wide[...], feat[z], preferred_element_type=F32)
            active = [jax.nn.sigmoid(logits[k * NX : (k + 1) * NX] + biases[k]) for k in range(6)]
            summed = active[0]
            for k in range(1, 6):
                summed = summed + active[k]
            inverse = 1.0 / (summed + 1.0)
            coupling = [active[k] * inverse for k in range(6)]
            for k in range(6):
                act[z, k] = active[k]
                kap[z + 1, k, :NX] = coupling[k]
            inv[z] = inverse
            sk[0, z, :NX] = packed(coupling)

        over_z(head)
        send(row_copies(2, 2, k_rows))
        send(strip_copies(1, sk))
        outermost = send(far_copies(3, g_rows, far_g) + far_copies(4, k_rows, far_k), awaited=False)
        for copy in arriving:
            copy.wait_recv()

        def clear(rows):
            hs[0, 1 : zs + 1, :chans, rows] = jnp.zeros((zs, chans, 4, NY), F32)
            kap[1 : zs + 1, :6, rows] = jnp.zeros((zs, 6, 4, NY), F32)

        @pl.when(me_x == gx - 1)
        def _():
            clear(slice(NX, NX + 4))

        @pl.when(me_x == 0)
        def _():
            clear(slice(NX + 4, RING))

        def assemble(z):
            hs[0, z + 1, chans] = unpacked(sf[0, z], sf[1, z], sf[2, z], 0)
            gs[0, z + 1, chans] = unpacked(sf[0, z], sf[1, z], sf[2, z], 8)
            flat[pl.ds(z * RING, RING)] = unpacked(sk[0, z], sk[1, z], sk[2, z], 0)

        over_z(assemble)
        strips = jnp.dot(
            flat[...], expand[...], precision=lax.Precision.HIGHEST, preferred_element_type=F32
        )
        for z in range(zs):
            for coefs, value in (
                (kst, [strips[z * RING : (z + 1) * RING, k * NY : (k + 1) * NY] for k in range(6)]),
                (kap, [kap[z + 1, k] for k in range(6)]),
            ):
                centre = 1.0
                for k in range(6):
                    centre = centre - value[k]
                    if coefs is kst:
                        coefs[z + 1, k] = value[k]
                coefs[z + 1, 6] = centre

        def columns(strip, j):
            return jnp.stack(
                [
                    jnp.broadcast_to(strip[:, c * EDGE + j : c * EDGE + j + 1], strip.shape)
                    for c in range(chans)
                ]
            )

        def around(rnd, z, rows):
            h, strip = hs[rnd, z + 1, :chans], hs[rnd, z + 1, chans, :rows]
            shape = (chans, rows, NY)
            lanes = iota(shape, 2)
            centre = h[:, :rows]
            return centre, [
                pltpu.roll(h, RING - 1, 1)[:, :rows],
                pltpu.roll(h, 1, 1)[:, :rows],
                jnp.where(lanes == NY - 1, columns(strip, HIGH), pltpu.roll(centre, NY - 1, 2)),
                jnp.where(lanes == 0, columns(strip, LOW), pltpu.roll(centre, 1, 2)),
                hs[rnd, z + 2, :chans, :rows],
                hs[rnd, z, :chans, :rows],
            ]

        def forward(rnd, z):
            h, beside = around(rnd, z, RING)
            result = kap[z + 1, 6] * h
            for k in range(6):
                result = result + kap[z + 1, k] * beside[k]
            strip = hs[rnd, z + 1, chans]
            edge = kst[z + 1, 6] * strip
            for k, value in enumerate((
                pltpu.roll(strip, RING - 1, 0),
                pltpu.roll(strip, 1, 0),
                pltpu.roll(strip, NY - 1, 1),
                pltpu.roll(strip, 1, 1),
                hs[rnd, z + 2, chans],
                hs[rnd, z, chans],
            )):
                edge = edge + kst[z + 1, k] * value
            hs[rnd + 1, z + 1, :chans] = result
            hs[rnd + 1, z + 1, chans] = edge

        def backward(rnd, z, rows):
            g, strip = gs[rnd, z + 1, :chans], gs[rnd, z + 1, chans]
            lanes = iota((chans, rows, NY), 2)
            near = g[:, :rows]
            edge = [kst[z + 1, k] * strip for k in range(4)]
            result = kap[z + 1, 6, :rows] * near
            result = result + pltpu.roll(kap[z + 1, 0] * g, 1, 1)[:, :rows]
            result = result + pltpu.roll(kap[z + 1, 1] * g, RING - 1, 1)[:, :rows]
            result = result + jnp.where(
                lanes == 0,
                columns(edge[2][:rows], LOW),
                pltpu.roll(kap[z + 1, 2, :rows] * near, 1, 2),
            )
            result = result + jnp.where(
                lanes == NY - 1,
                columns(edge[3][:rows], HIGH),
                pltpu.roll(kap[z + 1, 3, :rows] * near, NY - 1, 2),
            )
            result = result + kap[z, 4, :rows] * gs[rnd, z, :chans, :rows]
            result = result + kap[z + 2, 5, :rows] * gs[rnd, z + 2, :chans, :rows]
            if rows == NX:
                return result
            strip = kst[z + 1, 6] * strip
            strip = strip + pltpu.roll(edge[0], 1, 0) + pltpu.roll(edge[1], RING - 1, 0)
            strip = strip + pltpu.roll(edge[2], 1, 1) + pltpu.roll(edge[3], NY - 1, 1)
            strip = strip + kst[z, 4] * gs[rnd, z, chans] + kst[z + 2, 5] * gs[rnd, z + 2, chans]
            gs[rnd + 1, z + 1, :chans] = result
            gs[rnd + 1, z + 1, chans] = strip

        for rnd in range(ITERS - 1):

            def advance(z, rnd=rnd):
                forward(rnd, z)
                backward(rnd, z, RING)

            over_z(advance)

        bias_acc[...] = jnp.zeros((6, NX, NY), F32)

        def slopes(z):
            parts = [jnp.zeros((NX, NY), F32) for _ in range(7)]
            for rnd in range(ITERS):
                g = gs[ITERS - 1 - rnd, z + 1, :chans, :NX]
                h, beside = around(rnd, z, NX)
                for k in range(6):
                    parts[k] = parts[k] + jnp.sum(g * beside[k], 0)
                parts[6] = parts[6] + jnp.sum(g * h, 0)
            inner_sum = jnp.zeros((NX, NY), F32)
            effective = []
            for k in range(6):
                value = parts[k] - parts[6]
                effective.append(value)
                inner_sum = inner_sum + value * kap[z + 1, k, :NX]
            pieces = []
            for k in range(6):
                active = act[z, k]
                slope = (effective[k] - inner_sum) * inv[z] * active * (1.0 - active)
                bias_acc[k] += slope
                pieces.append(slope)
            dlow[z] = jnp.concatenate(pieces, axis=0).astype(BF16)

        over_z(slopes)

        cells = feats * NX
        total = jnp.zeros((cells, 6 * NX), F32)
        for z in range(0, zs, 2):
            total = total + lax.dot_general(
                jnp.concatenate([feat[z], feat[z + 1]], axis=1),
                jnp.concatenate([dlow[z], dlow[z + 1]], axis=1),
                (((1,), (1,)), ((), ())),
                preferred_element_type=F32,
            )
        total = jnp.where((iota((cells, 6 * NX), 0) & 7) == (iota((cells, 6 * NX), 1) & 7), total, 0.0)
        over_f = ((iota((2 * feats, cells), 1) >> 3) == iota((2 * feats, cells), 0)).astype(F32)
        over_k = ((iota((8, 6 * NX), 1) >> 3) == iota((8, 6 * NX), 0)).astype(F32)
        by_f = jnp.dot(over_f, total, precision=lax.Precision.HIGHEST, preferred_element_type=F32)
        by_f = lax.dot_general(
            over_k, by_f, (((1,), (1,)), ((), ())),
            precision=lax.Precision.HIGHEST, preferred_element_type=F32,
        )
        lane_row = iota((1, NY), 1)
        payload = [
            jnp.where(
                lane_row < feats,
                by_f[2 * r : 2 * r + 1],
                pltpu.roll(by_f[2 * r + 1 : 2 * r + 2], feats, 1),
            )
            for r in range(3)
        ]
        bias_row = jnp.zeros((1, NY), F32)
        for k in range(6):
            amount = jnp.sum(jnp.sum(bias_acc[k], 0, keepdims=True), 1, keepdims=True)
            bias_row = jnp.where(lane_row == k, amount, bias_row)
        payload = jnp.concatenate(payload + [bias_row], axis=0)

        def exchange(buffer, me, partners, send_sem, recv_sem, value):
            buffer[me] = value
            copies = [
                remote(buffer.at[me], buffer.at[me], send_sem.at[d], recv_sem.at[d], partner)
                for d, partner in enumerate(partners)
            ]
            for copy in copies:
                copy.start()
            pending.extend(copies)
            return copies

        def gather(buffer, copies, count):
            for copy in copies:
                copy.wait_recv()
            value = buffer[0]
            for i in range(1, count):
                value = value + buffer[i]
            return value

        first = exchange(sum_a, me_y, partners_a, sa_sem, ra_sem, payload)

        for copy in outermost:
            copy.wait_recv()

        def widen(z):
            for i, (known, row) in enumerate(((has_left, RING - 3), (has_right, NX + 2))):
                gs[0, z + 1, :chans, row : row + 1] = far_g[i, z, :, :1]
                kap[z + 1, :6, row : row + 1] = jnp.where(known, far_k[i, z, :, :1], 0.0)
            centre = 1.0
            for k in range(6):
                centre = centre - kap[z + 1, k, NX:]
            kap[z + 1, 6, NX:] = centre

        over_z(widen)
        for rnd in range(ITERS - 1):
            over_z(lambda z, rnd=rnd: backward(rnd, z, RING))

        def finish(z):
            g_out[z] = backward(ITERS - 1, z, NX)

        over_z(finish)
        store = pltpu.make_async_copy(g_out, out_hbm, local_sem.at[2 + zs])
        store.start()

        value = gather(sum_a, first, gy)
        second = exchange(sum_b, me_in, partners_b, sb_sem, rb_sem, value)
        value = gather(sum_b, second, inner)
        third = exchange(sum_c, me_out, partners_c, sc_sem, rc_sem, value)
        sum_ref[...] = gather(sum_c, third, outer) * factor
        for copy in pending:
            copy.wait_send()
        store.wait()

    return kernel


def deliver(feats):
    def kernel(field, sums, grad_probs, grad_weight, grad_bias, held, sems):
        planes = range(field.shape[0])
        loads = [pltpu.make_async_copy(field.at[z], held.at[z], sems.at[0, z]) for z in planes]
        stores = [pltpu.make_async_copy(held.at[z], grad_probs.at[z], sems.at[1, z]) for z in planes]
        for load in loads:
            load.start()
        for k in range(6):
            row = sums[k // 2 : k // 2 + 1, :]
            if k % 2:
                row = pltpu.roll(row, feats, 1)
            grad_weight[k : k + 1, :] = row[:, :feats]
        grad_bias[...] = sums[3:4, :6]
        for load, store in zip(loads, stores):
            load.wait()
            store.start()
        for store in stores:
            store.wait()

    return kernel


def inner_of(gx):
    return 8 if gx == 64 else 2


def per_device(features, head_weight, head_bias, probs, cotangent):
    zs, feats, nx, ny = features.shape
    chans = probs.shape[1]
    gx, gy = lax.axis_size("gx"), lax.axis_size("gy")
    inner = inner_of(gx)
    outer = gx // inner
    factor = 1.0 / math.sqrt(zs * nx * ny * gx * gy)
    dma = pltpu.SemaphoreType.DMA
    hbm = pl.BlockSpec(memory_space=pltpu.HBM)
    vmem = pl.BlockSpec(memory_space=pltpu.VMEM)
    field = pltpu.VMEM((ITERS, zs + 2, chans + 1, RING, ny), F32)
    coefs = pltpu.VMEM((zs + 2, 7, RING, ny), F32)
    grad_field, sums = pl.pallas_call(
        make_kernel(zs, chans, feats, gx, gy, inner, factor),
        out_shape=(
            jax.ShapeDtypeStruct(probs.shape, F32),
            jax.ShapeDtypeStruct((4, ny), F32),
        ),
        in_specs=[hbm, vmem, pl.BlockSpec(memory_space=pltpu.SMEM), hbm, hbm],
        out_specs=(hbm, vmem),
        scratch_shapes=[
            pltpu.VMEM((zs, feats * nx, ny), BF16),
            field,
            field,
            pltpu.VMEM((zs, chans, nx, ny), F32),
            coefs,
            coefs,
            pltpu.VMEM((zs, 6, nx, ny), F32),
            pltpu.VMEM((zs, nx, ny), F32),
            pltpu.VMEM((zs, 6 * nx, ny), BF16),
            pltpu.VMEM((6, nx, ny), F32),
            pltpu.VMEM((6 * nx, feats * nx), BF16),
            pltpu.VMEM((ny, 6 * ny), F32),
            pltpu.VMEM((3, zs, RING, ny), F32),
            pltpu.VMEM((3, zs, RING, ny), F32),
            pltpu.VMEM((zs * RING, ny), F32),
            pltpu.VMEM((2, zs, chans, nx, ny), F32),
            pltpu.VMEM((2, zs, 6, nx, ny), F32),
            pltpu.VMEM((gy, 4, ny), F32),
            pltpu.VMEM((inner, 4, ny), F32),
            pltpu.VMEM((outer, 4, ny), F32),
            dma((3 + zs,)),
            dma((5, 2)),
            dma((5, 2)),
            dma((2, len(SIDES))),
            dma((2, len(SIDES))),
            dma((gy - 1,)),
            dma((gy - 1,)),
            dma((inner - 1,)),
            dma((inner - 1,)),
            dma((outer - 1,)),
            dma((outer - 1,)),
        ],
        compiler_params=pltpu.CompilerParams(
            collective_id=0, has_side_effects=True, vmem_limit_bytes=63 * 1024 * 1024
        ),
        name="spread_backward",
    )(features.reshape(zs, feats * nx, ny), head_weight, head_bias, probs, cotangent)
    grad_probs, grad_weight, grad_bias = pl.pallas_call(
        deliver(feats),
        out_shape=(
            jax.ShapeDtypeStruct(probs.shape, F32),
            jax.ShapeDtypeStruct((6, feats), F32),
            jax.ShapeDtypeStruct((1, 6), F32),
        ),
        in_specs=[hbm, vmem],
        out_specs=(hbm, vmem, vmem),
        scratch_shapes=[pltpu.VMEM(probs.shape, F32), dma((2, zs))],
        name="deliver",
    )(grad_field, sums)
    return grad_probs, grad_weight, grad_bias.reshape(6)


def solution(mesh):
    spec = P(None, None, "gx", "gy")
    return jax.shard_map(
        per_device,
        mesh=mesh,
        in_specs=(spec, P(), P(), spec, spec),
        out_specs=(spec, P(), P()),
        check_vma=False,
    )
```

```python
import math

import jax
import jax.numpy as jnp
from jax import lax
from jax.experimental import pallas as pl
from jax.experimental.pallas import tpu as pltpu
from jax.sharding import PartitionSpec as P

F32 = jnp.float32
BF16 = jnp.bfloat16
MESH = pl.DeviceIdType.MESH
ITERS = 3
NX, NY = 8, 128
RING = 16
EDGE = 16
LOW, HIGH = 3, 12
SIDES = [(dx, dy) for dx in (1, -1, 0) for dy in (0, 1, -1) if dx or dy]


def iota(shape, dim):
    return lax.broadcasted_iota(jnp.int32, shape, dim)


def rows_of(dx, count):
    if dx == 0:
        return pl.ds(0, NX), pl.ds(0, NX)
    if dx > 0:
        return pl.ds(NX - count, count), pl.ds(RING - count, count)
    return pl.ds(0, count), pl.ds(NX, count)


def make_kernel(zs, chans, feats, gx, gy, inner, factor):
    outer = gx // inner
    inside = pl.ds(1, zs)

    def kernel(
        feat_hbm, weight_ref, bias_ref, probs_hbm, cot_hbm,
        out_hbm, sum_ref,
        feat, hs, gs, g_out, kap, kst, act, inv, dlow, bias_acc, wide, expand,
        sf, sk, flat, far_g, far_k, sum_a, sum_b, sum_c,
        local_sem, row_send, row_recv, strip_send, strip_recv,
        sa_sem, ra_sem, sb_sem, rb_sem, sc_sem, rc_sem,
    ):
        me_x, me_y = lax.axis_index("gx"), lax.axis_index("gy")
        me_in, me_out = lax.rem(me_x, inner), lax.div(me_x, inner)

        def at(dx, dy):
            return lax.rem(me_x + dx + gx, gx), lax.rem(me_y + dy + gy, gy)

        partners_a = [(me_x, lax.rem(me_y + d, gy)) for d in range(1, gy)]
        partners_b = [(me_out * inner + lax.rem(me_in + d, inner), me_y) for d in range(1, inner)]
        partners_c = [(lax.rem(me_out + d, outer) * inner + me_in, me_y) for d in range(1, outer)]
        greeted = [at(dx, dy) for dx, dy in SIDES if dx] + partners_a + partners_b + partners_c
        fields_in = [
            pltpu.make_async_copy(source, field.at[0, inside, pl.ds(0, chans), pl.ds(0, NX)], local_sem.at[i])
            for i, (source, field) in enumerate(((probs_hbm, hs), (cot_hbm, gs)))
        ]
        feats_in = [
            pltpu.make_async_copy(feat_hbm.at[z], feat.at[z], local_sem.at[2 + z]) for z in range(zs)
        ]
        for load in fields_in:
            load.start()
        barrier = pltpu.get_barrier_semaphore()
        for partner in greeted:
            pl.semaphore_signal(barrier, inc=1, device_id=partner, device_id_type=MESH)
        for load in feats_in:
            load.start()

        for field in (hs, gs):
            for step in range(ITERS):
                for z in (0, zs + 1):
                    field[step, z] = jnp.zeros((chans + 1, RING, NY), F32)
        for coefs in (kap, kst):
            for z in (0, zs + 1):
                coefs[z] = jnp.zeros((7, RING, NY), F32)

        spread = (iota((feats, feats * NX), 1) >> 3) == iota((feats, feats * NX), 0)
        same_x = (iota((6 * NX, feats * NX), 1) & 7) == (iota((6 * NX, feats * NX), 0) & 7)
        weight = weight_ref[...].astype(F32)
        rows = jnp.concatenate(
            [jnp.broadcast_to(weight[k : k + 1, :], (NX, feats)) for k in range(6)], axis=0
        )
        tall = jnp.dot(
            rows.astype(BF16), spread.astype(F32).astype(BF16), preferred_element_type=F32
        )
        wide[...] = jnp.where(same_x, tall, 0.0).astype(BF16)
        here, there = iota((NY, 6 * NY), 0), iota((NY, 6 * NY), 1)
        expand[...] = (((here >> 4) == (there >> 7)) & ((here & 15) == (there & 15))).astype(F32)

        lane = iota((NX, NY), 1)
        lane_j = lane & (EDGE - 1)
        ring_lane = iota((RING, NY), 1)
        ring_j = ring_lane & (EDGE - 1)
        ring_row = iota((RING, NY), 0)
        has_right, has_left = me_x < gx - 1, me_x > 0
        has_up, has_down = me_y < gy - 1, me_y > 0

        def packed(values):
            tile = jnp.zeros((NX, NY), F32)
            for i, value in enumerate(values):
                tile = jnp.where((lane >> 4) == i, pltpu.roll(value, i * EDGE + 4, 1), tile)
            return jnp.where(lane_j < 8, tile, 0.0)

        def unpacked(own, low, high, first):
            seen = (
                (ring_row < NX) | ((ring_row < NX + 4) & has_right) | ((ring_row >= NX + 4) & has_left)
            )
            low = jnp.where(has_down, low, 0.0)
            high = jnp.where(has_up, high, 0.0)
            near = jnp.where(ring_j < first + 4, low, own)
            far = jnp.where(ring_j < first + 4, own, high)
            if first:
                near = pltpu.roll(near, NY - first, 1)
            else:
                far = pltpu.roll(far, 8, 1)
            return jnp.where(seen, jnp.where(ring_j < 8, near, far), 0.0)

        def over_z(body):
            def run(z, carry):
                body(z)
                return carry

            lax.fori_loop(0, zs, run, 0, unroll=True)

        def remote(source, target, send_sem, recv_sem, device):
            return pltpu.make_async_remote_copy(
                src_ref=source, dst_ref=target, send_sem=send_sem, recv_sem=recv_sem,
                device_id=device, device_id_type=MESH,
            )

        pending, arriving = [], []

        def send(copies, awaited=True):
            for copy in copies:
                copy.start()
            pending.extend(copies)
            if awaited:
                arriving.extend(copies)
            return copies

        def row_copies(which, count, source, target):
            return [
                remote(
                    source(rows_of(dx, count)[0]), target(rows_of(dx, count)[1]),
                    row_send.at[which, i], row_recv.at[which, i], at(dx, 0),
                )
                for i, dx in enumerate((1, -1))
            ]

        def far_copies(which, view, target):
            return [
                remote(
                    view(pl.ds(row, 1)), target.at[i, pl.ds(0, zs), pl.ds(0, target.shape[2]), pl.ds(0, 1)],
                    row_send.at[which, i], row_recv.at[which, i], at(dx, 0),
                )
                for i, (dx, row) in enumerate(((1, NX - 3), (-1, 2)))
            ]

        def strip_copies(which, strip):
            return [
                remote(
                    strip.at[0, pl.ds(0, zs), rows_of(dx, 3)[0]],
                    strip.at[(0, 1, 2)[dy], pl.ds(0, zs), rows_of(dx, 3)[1]],
                    strip_send.at[which, i], strip_recv.at[which, i], at(dx, dy),
                )
                for i, (dx, dy) in enumerate(SIDES)
            ]

        pl.semaphore_wait(barrier, len(greeted))
        planes, every = pl.ds(0, zs), pl.ds(0, chans)
        send(row_copies(0, 3, lambda r: probs_hbm.at[planes, every, r], lambda r: hs.at[0, inside, every, r]))
        send(row_copies(1, 2, lambda r: cot_hbm.at[planes, every, r], lambda r: gs.at[0, inside, every, r]))
        for load in fields_in:
            load.wait()

        def pack_fields(z):
            of_h = packed([hs[0, z + 1, c, :NX] for c in range(chans)])
            of_g = packed([gs[0, z + 1, c, :NX] for c in range(chans)])
            sf[0, z, :NX] = of_h + pltpu.roll(of_g, 8, 1)

        over_z(pack_fields)
        send(strip_copies(0, sf))

        biases = [bias_ref[k] for k in range(6)]
        for load in feats_in:
            load.wait()

        def head(z):
            logits = jnp.dot(wide[...], feat[z], preferred_element_type=F32)
            active = [jax.nn.sigmoid(logits[k * NX : (k + 1) * NX] + biases[k]) for k in range(6)]
            summed = active[0]
            for k in range(1, 6):
                summed = summed + active[k]
            inverse = 1.0 / (summed + 1.0)
            coupling = [active[k] * inverse for k in range(6)]
            for k in range(6):
                act[z, k] = active[k]
                kap[z + 1, k, :NX] = coupling[k]
            inv[z] = inverse
            sk[0, z, :NX] = packed(coupling)

        over_z(head)
        k_rows = lambda r: kap.at[inside, pl.ds(0, 6), r]
        send(row_copies(2, 2, k_rows, k_rows))
        send(strip_copies(1, sk))
        outermost = send(
            far_copies(3, lambda r: cot_hbm.at[planes, every, r], far_g)
            + far_copies(4, k_rows, far_k),
            awaited=False,
        )
        for copy in arriving:
            copy.wait_recv()

        def clear(rows):
            hs[0, 1 : zs + 1, :chans, rows] = jnp.zeros((zs, chans, 4, NY), F32)
            kap[1 : zs + 1, :6, rows] = jnp.zeros((zs, 6, 4, NY), F32)

        @pl.when(me_x == gx - 1)
        def _():
            clear(slice(NX, NX + 4))

        @pl.when(me_x == 0)
        def _():
            clear(slice(NX + 4, RING))

        def assemble(z):
            hs[0, z + 1, chans] = unpacked(sf[0, z], sf[1, z], sf[2, z], 0)
            gs[0, z + 1, chans] = unpacked(sf[0, z], sf[1, z], sf[2, z], 8)
            flat[pl.ds(z * RING, RING)] = unpacked(sk[0, z], sk[1, z], sk[2, z], 0)

        over_z(assemble)
        strips = jnp.dot(
            flat[...], expand[...], precision=lax.Precision.HIGHEST, preferred_element_type=F32
        )
        for z in range(zs):
            for coefs, value in (
                (kst, [strips[z * RING : (z + 1) * RING, k * NY : (k + 1) * NY] for k in range(6)]),
                (kap, [kap[z + 1, k] for k in range(6)]),
            ):
                centre = 1.0
                for k in range(6):
                    centre = centre - value[k]
                    if coefs is kst:
                        coefs[z + 1, k] = value[k]
                coefs[z + 1, 6] = centre

        def columns(strip, j):
            return jnp.stack(
                [
                    jnp.broadcast_to(strip[:, c * EDGE + j : c * EDGE + j + 1], strip.shape)
                    for c in range(chans)
                ]
            )

        def around(rnd, z, rows):
            h, strip = hs[rnd, z + 1, :chans], hs[rnd, z + 1, chans, :rows]
            shape = (chans, rows, NY)
            lanes = iota(shape, 2)
            centre = h[:, :rows]
            return centre, [
                pltpu.roll(h, RING - 1, 1)[:, :rows],
                pltpu.roll(h, 1, 1)[:, :rows],
                jnp.where(lanes == NY - 1, columns(strip, HIGH), pltpu.roll(centre, NY - 1, 2)),
                jnp.where(lanes == 0, columns(strip, LOW), pltpu.roll(centre, 1, 2)),
                hs[rnd, z + 2, :chans, :rows],
                hs[rnd, z, :chans, :rows],
            ]

        def forward(rnd, z):
            h, beside = around(rnd, z, RING)
            result = kap[z + 1, 6] * h
            for k in range(6):
                result = result + kap[z + 1, k] * beside[k]
            strip = hs[rnd, z + 1, chans]
            edge = kst[z + 1, 6] * strip
            for k, value in enumerate((
                pltpu.roll(strip, RING - 1, 0),
                pltpu.roll(strip, 1, 0),
                pltpu.roll(strip, NY - 1, 1),
                pltpu.roll(strip, 1, 1),
                hs[rnd, z + 2, chans],
                hs[rnd, z, chans],
            )):
                edge = edge + kst[z + 1, k] * value
            hs[rnd + 1, z + 1, :chans] = result
            hs[rnd + 1, z + 1, chans] = edge

        def backward(rnd, z, rows):
            g, strip = gs[rnd, z + 1, :chans], gs[rnd, z + 1, chans]
            lanes = iota((chans, rows, NY), 2)
            near = g[:, :rows]
            edge = [kst[z + 1, k] * strip for k in range(4)]
            result = kap[z + 1, 6, :rows] * near
            result = result + pltpu.roll(kap[z + 1, 0] * g, 1, 1)[:, :rows]
            result = result + pltpu.roll(kap[z + 1, 1] * g, RING - 1, 1)[:, :rows]
            result = result + jnp.where(
                lanes == 0,
                columns(edge[2][:rows], LOW),
                pltpu.roll(kap[z + 1, 2, :rows] * near, 1, 2),
            )
            result = result + jnp.where(
                lanes == NY - 1,
                columns(edge[3][:rows], HIGH),
                pltpu.roll(kap[z + 1, 3, :rows] * near, NY - 1, 2),
            )
            result = result + kap[z, 4, :rows] * gs[rnd, z, :chans, :rows]
            result = result + kap[z + 2, 5, :rows] * gs[rnd, z + 2, :chans, :rows]
            if rows == NX:
                return result
            strip = kst[z + 1, 6] * strip
            strip = strip + pltpu.roll(edge[0], 1, 0) + pltpu.roll(edge[1], RING - 1, 0)
            strip = strip + pltpu.roll(edge[2], 1, 1) + pltpu.roll(edge[3], NY - 1, 1)
            strip = strip + kst[z, 4] * gs[rnd, z, chans] + kst[z + 2, 5] * gs[rnd, z + 2, chans]
            gs[rnd + 1, z + 1, :chans] = result
            gs[rnd + 1, z + 1, chans] = strip

        for rnd in range(ITERS - 1):

            def advance(z, rnd=rnd):
                forward(rnd, z)
                backward(rnd, z, RING)

            over_z(advance)

        bias_acc[...] = jnp.zeros((6, NX, NY), F32)

        def slopes(z):
            parts = [jnp.zeros((NX, NY), F32) for _ in range(7)]
            for rnd in range(ITERS):
                g = gs[ITERS - 1 - rnd, z + 1, :chans, :NX]
                h, beside = around(rnd, z, NX)
                for k in range(6):
                    parts[k] = parts[k] + jnp.sum(g * beside[k], 0)
                parts[6] = parts[6] + jnp.sum(g * h, 0)
            inner_sum = jnp.zeros((NX, NY), F32)
            effective = []
            for k in range(6):
                value = parts[k] - parts[6]
                effective.append(value)
                inner_sum = inner_sum + value * kap[z + 1, k, :NX]
            pieces = []
            for k in range(6):
                active = act[z, k]
                slope = (effective[k] - inner_sum) * inv[z] * active * (1.0 - active)
                bias_acc[k] += slope
                pieces.append(slope)
            dlow[z] = jnp.concatenate(pieces, axis=0).astype(BF16)

        over_z(slopes)

        cells = feats * NX
        total = jnp.zeros((cells, 6 * NX), F32)
        for z in range(0, zs, 2):
            total = total + lax.dot_general(
                jnp.concatenate([feat[z], feat[z + 1]], axis=1),
                jnp.concatenate([dlow[z], dlow[z + 1]], axis=1),
                (((1,), (1,)), ((), ())),
                preferred_element_type=F32,
            )
        total = jnp.where((iota((cells, 6 * NX), 0) & 7) == (iota((cells, 6 * NX), 1) & 7), total, 0.0)
        over_f = ((iota((2 * feats, cells), 1) >> 3) == iota((2 * feats, cells), 0)).astype(F32)
        over_k = ((iota((8, 6 * NX), 1) >> 3) == iota((8, 6 * NX), 0)).astype(F32)
        by_f = jnp.dot(over_f, total, precision=lax.Precision.HIGHEST, preferred_element_type=F32)
        by_f = lax.dot_general(
            over_k, by_f, (((1,), (1,)), ((), ())),
            precision=lax.Precision.HIGHEST, preferred_element_type=F32,
        )
        lane_row = iota((1, NY), 1)
        payload = [
            jnp.where(
                lane_row < feats,
                by_f[2 * r : 2 * r + 1],
                pltpu.roll(by_f[2 * r + 1 : 2 * r + 2], feats, 1),
            )
            for r in range(3)
        ]
        bias_row = jnp.zeros((1, NY), F32)
        for k in range(6):
            amount = jnp.sum(jnp.sum(bias_acc[k], 0, keepdims=True), 1, keepdims=True)
            bias_row = jnp.where(lane_row == k, amount, bias_row)
        payload = jnp.concatenate(payload + [bias_row], axis=0)

        def exchange(buffer, me, partners, send_sem, recv_sem, value):
            buffer[me] = value
            copies = [
                remote(buffer.at[me], buffer.at[me], send_sem.at[d], recv_sem.at[d], partner)
                for d, partner in enumerate(partners)
            ]
            for copy in copies:
                copy.start()
            pending.extend(copies)
            return copies

        def gather(buffer, copies, count):
            for copy in copies:
                copy.wait_recv()
            value = buffer[0]
            for i in range(1, count):
                value = value + buffer[i]
            return value

        first = exchange(sum_c, me_out, partners_c, sc_sem, rc_sem, payload)

        for copy in outermost:
            copy.wait_recv()

        def widen(z):
            for i, (known, row) in enumerate(((has_left, RING - 3), (has_right, NX + 2))):
                gs[0, z + 1, :chans, row : row + 1] = far_g[i, z, :, :1]
                kap[z + 1, :6, row : row + 1] = jnp.where(known, far_k[i, z, :, :1], 0.0)
            centre = 1.0
            for k in range(6):
                centre = centre - kap[z + 1, k, NX:]
            kap[z + 1, 6, NX:] = centre

        over_z(widen)
        over_z(lambda z: backward(0, z, RING))
        value = gather(sum_c, first, outer)
        second = exchange(sum_a, me_y, partners_a, sa_sem, ra_sem, value)
        over_z(lambda z: backward(1, z, RING))

        def finish(z):
            g_out[z] = backward(ITERS - 1, z, NX)

        over_z(finish)
        store = pltpu.make_async_copy(g_out, out_hbm, local_sem.at[2 + zs])
        store.start()
        value = gather(sum_a, second, gy)
        third = exchange(sum_b, me_in, partners_b, sb_sem, rb_sem, value)
        sum_ref[...] = gather(sum_b, third, inner) * factor
        for copy in pending:
            copy.wait_send()
        store.wait()

    return kernel


def deliver(feats):
    def kernel(field, sums, grad_probs, grad_weight, grad_bias, held, sums_in, weight_out, bias_out, sems, small):
        planes = range(field.shape[0])
        loads = [pltpu.make_async_copy(field.at[z], held.at[z], sems.at[0, z]) for z in planes]
        stores = [pltpu.make_async_copy(held.at[z], grad_probs.at[z], sems.at[1, z]) for z in planes]
        first = pltpu.make_async_copy(sums, sums_in, small.at[0])
        last = [
            pltpu.make_async_copy(weight_out, grad_weight, small.at[1]),
            pltpu.make_async_copy(bias_out, grad_bias, small.at[2]),
        ]
        first.start()
        for load in loads:
            load.start()
        first.wait()
        for k in range(6):
            row = sums_in[k // 2 : k // 2 + 1, :]
            if k % 2:
                row = pltpu.roll(row, feats, 1)
            weight_out[k : k + 1, :] = row[:, :feats]
        bias_out[...] = sums_in[3:4, :6]
        for copy in last:
            copy.start()
        for load, store in zip(loads, stores):
            load.wait()
            store.start()
        for copy in stores + last:
            copy.wait()

    return kernel


def inner_of(gx):
    return 8 if gx == 64 else 2


def per_device(features, head_weight, head_bias, probs, cotangent):
    zs, feats, nx, ny = features.shape
    chans = probs.shape[1]
    gx, gy = lax.axis_size("gx"), lax.axis_size("gy")
    inner = inner_of(gx)
    outer = gx // inner
    factor = 1.0 / math.sqrt(zs * nx * ny * gx * gy)
    dma = pltpu.SemaphoreType.DMA
    hbm = pl.BlockSpec(memory_space=pltpu.HBM)
    vmem = pl.BlockSpec(memory_space=pltpu.VMEM)
    field = pltpu.VMEM((ITERS, zs + 2, chans + 1, RING, ny), F32)
    coefs = pltpu.VMEM((zs + 2, 7, RING, ny), F32)
    grad_field, sums = pl.pallas_call(
        make_kernel(zs, chans, feats, gx, gy, inner, factor),
        out_shape=(
            jax.ShapeDtypeStruct(probs.shape, F32),
            jax.ShapeDtypeStruct((4, ny), F32),
        ),
        in_specs=[hbm, vmem, pl.BlockSpec(memory_space=pltpu.SMEM), hbm, hbm],
        out_specs=(hbm, vmem),
        scratch_shapes=[
            pltpu.VMEM((zs, feats * nx, ny), BF16),
            field,
            field,
            pltpu.VMEM((zs, chans, nx, ny), F32),
            coefs,
            coefs,
            pltpu.VMEM((zs, 6, nx, ny), F32),
            pltpu.VMEM((zs, nx, ny), F32),
            pltpu.VMEM((zs, 6 * nx, ny), BF16),
            pltpu.VMEM((6, nx, ny), F32),
            pltpu.VMEM((6 * nx, feats * nx), BF16),
            pltpu.VMEM((ny, 6 * ny), F32),
            pltpu.VMEM((3, zs, RING, ny), F32),
            pltpu.VMEM((3, zs, RING, ny), F32),
            pltpu.VMEM((zs * RING, ny), F32),
            pltpu.VMEM((2, zs, chans, nx, ny), F32),
            pltpu.VMEM((2, zs, 6, nx, ny), F32),
            pltpu.VMEM((gy, 4, ny), F32),
            pltpu.VMEM((inner, 4, ny), F32),
            pltpu.VMEM((outer, 4, ny), F32),
            dma((3 + zs,)),
            dma((5, 2)),
            dma((5, 2)),
            dma((2, len(SIDES))),
            dma((2, len(SIDES))),
            dma((gy - 1,)),
            dma((gy - 1,)),
            dma((inner - 1,)),
            dma((inner - 1,)),
            dma((outer - 1,)),
            dma((outer - 1,)),
        ],
        compiler_params=pltpu.CompilerParams(
            collective_id=0, has_side_effects=True, vmem_limit_bytes=63 * 1024 * 1024
        ),
        name="spread_backward",
    )(features.reshape(zs, feats * nx, ny), head_weight, head_bias, probs, cotangent)
    grad_probs, grad_weight, grad_bias = pl.pallas_call(
        deliver(feats),
        out_shape=(
            jax.ShapeDtypeStruct(probs.shape, F32),
            jax.ShapeDtypeStruct((6, feats), F32),
            jax.ShapeDtypeStruct((1, 6), F32),
        ),
        in_specs=[hbm, hbm],
        out_specs=(hbm, hbm, hbm),
        scratch_shapes=[
            pltpu.VMEM(probs.shape, F32),
            pltpu.VMEM((4, ny), F32),
            pltpu.VMEM((6, feats), F32),
            pltpu.VMEM((1, 6), F32),
            dma((2, zs)),
            dma((3,)),
        ],
        name="deliver",
    )(grad_field, sums)
    return grad_probs, grad_weight, grad_bias.reshape(6)


def solution(mesh):
    spec = P(None, None, "gx", "gy")
    return jax.shard_map(
        per_device,
        mesh=mesh,
        in_specs=(spec, P(), P(), spec, spec),
        out_specs=(spec, P(), P()),
        check_vma=False,
    )
```

```python
import math

import jax
import jax.numpy as jnp
from jax import lax
from jax.experimental import pallas as pl
from jax.experimental.pallas import tpu as pltpu
from jax.sharding import PartitionSpec as P

F32 = jnp.float32
BF16 = jnp.bfloat16
MESH = pl.DeviceIdType.MESH
ITERS = 3
NX, NY = 8, 128
RING = 16
EDGE = 16
LOW, HIGH = 3, 12
SIDES = [(dx, dy) for dx in (1, -1, 0) for dy in (0, 1, -1) if dx or dy]


def iota(shape, dim):
    return lax.broadcasted_iota(jnp.int32, shape, dim)


def rows_of(dx, count):
    if dx == 0:
        return pl.ds(0, NX), pl.ds(0, NX)
    if dx > 0:
        return pl.ds(NX - count, count), pl.ds(RING - count, count)
    return pl.ds(0, count), pl.ds(NX, count)


def make_kernel(zs, chans, feats, gx, gy, inner, factor):
    outer = gx // inner
    inside = pl.ds(1, zs)

    def kernel(
        feat_hbm, weight_ref, bias_ref, probs_hbm, cot_hbm,
        out_hbm, sum_ref,
        feat, hs, gs, g_out, kap, kst, act, inv, dlow, bias_acc, wide, expand,
        sf, sk, flat, far_g, far_k, sum_a, sum_b, sum_c,
        local_sem, row_send, row_recv, strip_send, strip_recv,
        sa_sem, ra_sem, sb_sem, rb_sem, sc_sem, rc_sem,
    ):
        me_x, me_y = lax.axis_index("gx"), lax.axis_index("gy")
        me_in, me_out = lax.rem(me_x, inner), lax.div(me_x, inner)

        def at(dx, dy):
            return lax.rem(me_x + dx + gx, gx), lax.rem(me_y + dy + gy, gy)

        partners_a = [(me_x, lax.rem(me_y + d, gy)) for d in range(1, gy)]
        partners_b = [(me_out * inner + lax.rem(me_in + d, inner), me_y) for d in range(1, inner)]
        partners_c = [(lax.rem(me_out + d, outer) * inner + me_in, me_y) for d in range(1, outer)]
        greeted = [at(dx, dy) for dx, dy in SIDES if dx] + partners_a + partners_b + partners_c
        fields_in = [
            pltpu.make_async_copy(source, field.at[0, inside, pl.ds(0, chans), pl.ds(0, NX)], local_sem.at[i])
            for i, (source, field) in enumerate(((probs_hbm, hs), (cot_hbm, gs)))
        ]
        feats_in = [
            pltpu.make_async_copy(feat_hbm.at[z], feat.at[z], local_sem.at[2 + z]) for z in range(zs)
        ]
        for load in fields_in:
            load.start()
        barrier = pltpu.get_barrier_semaphore()
        for partner in greeted:
            pl.semaphore_signal(barrier, inc=1, device_id=partner, device_id_type=MESH)
        for load in feats_in:
            load.start()

        for field in (hs, gs):
            for step in range(ITERS):
                for z in (0, zs + 1):
                    field[step, z] = jnp.zeros((chans + 1, RING, NY), F32)
        for coefs in (kap, kst):
            for z in (0, zs + 1):
                coefs[z] = jnp.zeros((7, RING, NY), F32)

        spread = (iota((feats, feats * NX), 1) >> 3) == iota((feats, feats * NX), 0)
        same_x = (iota((6 * NX, feats * NX), 1) & 7) == (iota((6 * NX, feats * NX), 0) & 7)
        weight = weight_ref[...].astype(F32)
        rows = jnp.concatenate(
            [jnp.broadcast_to(weight[k : k + 1, :], (NX, feats)) for k in range(6)], axis=0
        )
        tall = jnp.dot(
            rows.astype(BF16), spread.astype(F32).astype(BF16), preferred_element_type=F32
        )
        wide[...] = jnp.where(same_x, tall, 0.0).astype(BF16)
        here, there = iota((NY, 6 * NY), 0), iota((NY, 6 * NY), 1)
        expand[...] = (((here >> 4) == (there >> 7)) & ((here & 15) == (there & 15))).astype(F32)

        lane = iota((NX, NY), 1)
        lane_j = lane & (EDGE - 1)
        ring_lane = iota((RING, NY), 1)
        ring_j = ring_lane & (EDGE - 1)
        ring_row = iota((RING, NY), 0)
        has_right, has_left = me_x < gx - 1, me_x > 0
        has_up, has_down = me_y < gy - 1, me_y > 0

        def packed(values):
            tile = jnp.zeros((NX, NY), F32)
            for i, value in enumerate(values):
                tile = jnp.where((lane >> 4) == i, pltpu.roll(value, i * EDGE + 4, 1), tile)
            return jnp.where(lane_j < 8, tile, 0.0)

        def unpacked(own, low, high, first):
            seen = (
                (ring_row < NX) | ((ring_row < NX + 4) & has_right) | ((ring_row >= NX + 4) & has_left)
            )
            low = jnp.where(has_down, low, 0.0)
            high = jnp.where(has_up, high, 0.0)
            near = jnp.where(ring_j < first + 4, low, own)
            far = jnp.where(ring_j < first + 4, own, high)
            if first:
                near = pltpu.roll(near, NY - first, 1)
            else:
                far = pltpu.roll(far, 8, 1)
            return jnp.where(seen, jnp.where(ring_j < 8, near, far), 0.0)

        def over_z(body):
            def run(z, carry):
                body(z)
                return carry

            lax.fori_loop(0, zs, run, 0, unroll=True)

        def remote(source, target, send_sem, recv_sem, device):
            return pltpu.make_async_remote_copy(
                src_ref=source, dst_ref=target, send_sem=send_sem, recv_sem=recv_sem,
                device_id=device, device_id_type=MESH,
            )

        pending, arriving = [], []

        def send(copies, awaited=True):
            for copy in copies:
                copy.start()
            pending.extend(copies)
            if awaited:
                arriving.extend(copies)
            return copies

        def row_copies(which, count, source, target):
            return [
                remote(
                    source(rows_of(dx, count)[0]), target(rows_of(dx, count)[1]),
                    row_send.at[which, i], row_recv.at[which, i], at(dx, 0),
                )
                for i, dx in enumerate((1, -1))
            ]

        def far_copies(which, view, target):
            return [
                remote(
                    view(pl.ds(row, 1)), target.at[i, pl.ds(0, zs), pl.ds(0, target.shape[2]), pl.ds(0, 1)],
                    row_send.at[which, i], row_recv.at[which, i], at(dx, 0),
                )
                for i, (dx, row) in enumerate(((1, NX - 3), (-1, 2)))
            ]

        def strip_copies(which, strip):
            return [
                remote(
                    strip.at[0, pl.ds(0, zs), rows_of(dx, 3)[0]],
                    strip.at[(0, 1, 2)[dy], pl.ds(0, zs), rows_of(dx, 3)[1]],
                    strip_send.at[which, i], strip_recv.at[which, i], at(dx, dy),
                )
                for i, (dx, dy) in enumerate(SIDES)
            ]

        for load in fields_in:
            load.wait()

        def pack_fields(z):
            of_h = packed([hs[0, z + 1, c, :NX] for c in range(chans)])
            of_g = packed([gs[0, z + 1, c, :NX] for c in range(chans)])
            sf[0, z, :NX] = of_h + pltpu.roll(of_g, 8, 1)

        over_z(pack_fields)
        pl.semaphore_wait(barrier, len(greeted))
        planes, every = pl.ds(0, zs), pl.ds(0, chans)
        send(row_copies(0, 3, lambda r: hs.at[0, inside, every, r], lambda r: hs.at[0, inside, every, r]))
        send(row_copies(1, 2, lambda r: gs.at[0, inside, every, r], lambda r: gs.at[0, inside, every, r]))
        send(strip_copies(0, sf))

        biases = [bias_ref[k] for k in range(6)]
        for load in feats_in:
            load.wait()

        def head(z):
            logits = jnp.dot(wide[...], feat[z], preferred_element_type=F32)
            active = [jax.nn.sigmoid(logits[k * NX : (k + 1) * NX] + biases[k]) for k in range(6)]
            summed = active[0]
            for k in range(1, 6):
                summed = summed + active[k]
            inverse = 1.0 / (summed + 1.0)
            coupling = [active[k] * inverse for k in range(6)]
            for k in range(6):
                act[z, k] = active[k]
                kap[z + 1, k, :NX] = coupling[k]
            inv[z] = inverse
            sk[0, z, :NX] = packed(coupling)

        over_z(head)
        k_rows = lambda r: kap.at[inside, pl.ds(0, 6), r]
        send(row_copies(2, 2, k_rows, k_rows))
        send(strip_copies(1, sk))
        outermost = send(
            far_copies(3, lambda r: gs.at[0, inside, every, r], far_g)
            + far_copies(4, k_rows, far_k),
            awaited=False,
        )
        for copy in arriving:
            copy.wait_recv()

        def clear(rows):
            hs[0, 1 : zs + 1, :chans, rows] = jnp.zeros((zs, chans, 4, NY), F32)
            kap[1 : zs + 1, :6, rows] = jnp.zeros((zs, 6, 4, NY), F32)

        @pl.when(me_x == gx - 1)
        def _():
            clear(slice(NX, NX + 4))

        @pl.when(me_x == 0)
        def _():
            clear(slice(NX + 4, RING))

        def assemble(z):
            hs[0, z + 1, chans] = unpacked(sf[0, z], sf[1, z], sf[2, z], 0)
            gs[0, z + 1, chans] = unpacked(sf[0, z], sf[1, z], sf[2, z], 8)
            flat[pl.ds(z * RING, RING)] = unpacked(sk[0, z], sk[1, z], sk[2, z], 0)

        over_z(assemble)
        strips = jnp.dot(
            flat[...], expand[...], precision=lax.Precision.HIGHEST, preferred_element_type=F32
        )
        for z in range(zs):
            for coefs, value in (
                (kst, [strips[z * RING : (z + 1) * RING, k * NY : (k + 1) * NY] for k in range(6)]),
                (kap, [kap[z + 1, k] for k in range(6)]),
            ):
                centre = 1.0
                for k in range(6):
                    centre = centre - value[k]
                    if coefs is kst:
                        coefs[z + 1, k] = value[k]
                coefs[z + 1, 6] = centre

        def columns(strip, j):
            return jnp.stack(
                [
                    jnp.broadcast_to(strip[:, c * EDGE + j : c * EDGE + j + 1], strip.shape)
                    for c in range(chans)
                ]
            )

        def around(rnd, z, rows):
            h, strip = hs[rnd, z + 1, :chans], hs[rnd, z + 1, chans, :rows]
            shape = (chans, rows, NY)
            lanes = iota(shape, 2)
            centre = h[:, :rows]
            return centre, [
                pltpu.roll(h, RING - 1, 1)[:, :rows],
                pltpu.roll(h, 1, 1)[:, :rows],
                jnp.where(lanes == NY - 1, columns(strip, HIGH), pltpu.roll(centre, NY - 1, 2)),
                jnp.where(lanes == 0, columns(strip, LOW), pltpu.roll(centre, 1, 2)),
                hs[rnd, z + 2, :chans, :rows],
                hs[rnd, z, :chans, :rows],
            ]

        def forward(rnd, z):
            h, beside = around(rnd, z, RING)
            result = kap[z + 1, 6] * h
            for k in range(6):
                result = result + kap[z + 1, k] * beside[k]
            strip = hs[rnd, z + 1, chans]
            edge = kst[z + 1, 6] * strip
            for k, value in enumerate((
                pltpu.roll(strip, RING - 1, 0),
                pltpu.roll(strip, 1, 0),
                pltpu.roll(strip, NY - 1, 1),
                pltpu.roll(strip, 1, 1),
                hs[rnd, z + 2, chans],
                hs[rnd, z, chans],
            )):
                edge = edge + kst[z + 1, k] * value
            hs[rnd + 1, z + 1, :chans] = result
            hs[rnd + 1, z + 1, chans] = edge

        def backward(rnd, z, rows):
            g, strip = gs[rnd, z + 1, :chans], gs[rnd, z + 1, chans]
            lanes = iota((chans, rows, NY), 2)
            near = g[:, :rows]
            edge = [kst[z + 1, k] * strip for k in range(4)]
            result = kap[z + 1, 6, :rows] * near
            result = result + pltpu.roll(kap[z + 1, 0] * g, 1, 1)[:, :rows]
            result = result + pltpu.roll(kap[z + 1, 1] * g, RING - 1, 1)[:, :rows]
            result = result + jnp.where(
                lanes == 0,
                columns(edge[2][:rows], LOW),
                pltpu.roll(kap[z + 1, 2, :rows] * near, 1, 2),
            )
            result = result + jnp.where(
                lanes == NY - 1,
                columns(edge[3][:rows], HIGH),
                pltpu.roll(kap[z + 1, 3, :rows] * near, NY - 1, 2),
            )
            result = result + kap[z, 4, :rows] * gs[rnd, z, :chans, :rows]
            result = result + kap[z + 2, 5, :rows] * gs[rnd, z + 2, :chans, :rows]
            if rows == NX:
                return result
            strip = kst[z + 1, 6] * strip
            strip = strip + pltpu.roll(edge[0], 1, 0) + pltpu.roll(edge[1], RING - 1, 0)
            strip = strip + pltpu.roll(edge[2], 1, 1) + pltpu.roll(edge[3], NY - 1, 1)
            strip = strip + kst[z, 4] * gs[rnd, z, chans] + kst[z + 2, 5] * gs[rnd, z + 2, chans]
            gs[rnd + 1, z + 1, :chans] = result
            gs[rnd + 1, z + 1, chans] = strip

        for rnd in range(ITERS - 1):

            def advance(z, rnd=rnd):
                forward(rnd, z)
                backward(rnd, z, RING)

            over_z(advance)

        bias_acc[...] = jnp.zeros((6, NX, NY), F32)

        def slopes(z):
            parts = [jnp.zeros((NX, NY), F32) for _ in range(7)]
            for rnd in range(ITERS):
                g = gs[ITERS - 1 - rnd, z + 1, :chans, :NX]
                h, beside = around(rnd, z, NX)
                for k in range(6):
                    parts[k] = parts[k] + jnp.sum(g * beside[k], 0)
                parts[6] = parts[6] + jnp.sum(g * h, 0)
            inner_sum = jnp.zeros((NX, NY), F32)
            effective = []
            for k in range(6):
                value = parts[k] - parts[6]
                effective.append(value)
                inner_sum = inner_sum + value * kap[z + 1, k, :NX]
            pieces = []
            for k in range(6):
                active = act[z, k]
                slope = (effective[k] - inner_sum) * inv[z] * active * (1.0 - active)
                bias_acc[k] += slope
                pieces.append(slope)
            dlow[z] = jnp.concatenate(pieces, axis=0).astype(BF16)

        over_z(slopes)

        cells = feats * NX
        total = jnp.zeros((cells, 6 * NX), F32)
        for z in range(0, zs, 2):
            total = total + lax.dot_general(
                jnp.concatenate([feat[z], feat[z + 1]], axis=1),
                jnp.concatenate([dlow[z], dlow[z + 1]], axis=1),
                (((1,), (1,)), ((), ())),
                preferred_element_type=F32,
            )
        total = jnp.where((iota((cells, 6 * NX), 0) & 7) == (iota((cells, 6 * NX), 1) & 7), total, 0.0)
        over_f = ((iota((2 * feats, cells), 1) >> 3) == iota((2 * feats, cells), 0)).astype(F32)
        over_k = ((iota((8, 6 * NX), 1) >> 3) == iota((8, 6 * NX), 0)).astype(F32)
        by_f = jnp.dot(over_f, total, precision=lax.Precision.HIGHEST, preferred_element_type=F32)
        by_f = lax.dot_general(
            over_k, by_f, (((1,), (1,)), ((), ())),
            precision=lax.Precision.HIGHEST, preferred_element_type=F32,
        )
        lane_row = iota((1, NY), 1)
        payload = [
            jnp.where(
                lane_row < feats,
                by_f[2 * r : 2 * r + 1],
                pltpu.roll(by_f[2 * r + 1 : 2 * r + 2], feats, 1),
            )
            for r in range(3)
        ]
        bias_row = jnp.zeros((1, NY), F32)
        for k in range(6):
            amount = jnp.sum(jnp.sum(bias_acc[k], 0, keepdims=True), 1, keepdims=True)
            bias_row = jnp.where(lane_row == k, amount, bias_row)
        payload = jnp.concatenate(payload + [bias_row], axis=0)

        def exchange(buffer, me, partners, send_sem, recv_sem, value):
            buffer[me] = value
            copies = [
                remote(buffer.at[me], buffer.at[me], send_sem.at[d], recv_sem.at[d], partner)
                for d, partner in enumerate(partners)
            ]
            for copy in copies:
                copy.start()
            pending.extend(copies)
            return copies

        def gather(buffer, copies, count):
            for copy in copies:
                copy.wait_recv()
            value = buffer[0]
            for i in range(1, count):
                value = value + buffer[i]
            return value

        first = exchange(sum_c, me_out, partners_c, sc_sem, rc_sem, payload)

        for copy in outermost:
            copy.wait_recv()

        def widen(z):
            for i, (known, row) in enumerate(((has_left, RING - 3), (has_right, NX + 2))):
                gs[0, z + 1, :chans, row : row + 1] = far_g[i, z, :, :1]
                kap[z + 1, :6, row : row + 1] = jnp.where(known, far_k[i, z, :, :1], 0.0)
            centre = 1.0
            for k in range(6):
                centre = centre - kap[z + 1, k, NX:]
            kap[z + 1, 6, NX:] = centre

        over_z(widen)
        over_z(lambda z: backward(0, z, RING))
        value = gather(sum_c, first, outer)
        second = exchange(sum_a, me_y, partners_a, sa_sem, ra_sem, value)
        over_z(lambda z: backward(1, z, RING))

        def finish(z):
            g_out[z] = backward(ITERS - 1, z, NX)

        over_z(finish)
        store = pltpu.make_async_copy(g_out, out_hbm, local_sem.at[2 + zs])
        store.start()
        value = gather(sum_a, second, gy)
        third = exchange(sum_b, me_in, partners_b, sb_sem, rb_sem, value)
        sum_ref[...] = gather(sum_b, third, inner) * factor
        for copy in pending:
            copy.wait_send()
        store.wait()

    return kernel


def deliver(feats):
    def kernel(field, sums, grad_probs, grad_weight, grad_bias, held, sums_in, weight_out, bias_out, sems, small):
        planes = range(field.shape[0])
        loads = [pltpu.make_async_copy(field.at[z], held.at[z], sems.at[0, z]) for z in planes]
        stores = [pltpu.make_async_copy(held.at[z], grad_probs.at[z], sems.at[1, z]) for z in planes]
        first = pltpu.make_async_copy(sums, sums_in, small.at[0])
        last = [
            pltpu.make_async_copy(weight_out, grad_weight, small.at[1]),
            pltpu.make_async_copy(bias_out, grad_bias, small.at[2]),
        ]
        first.start()
        for load in loads:
            load.start()
        first.wait()
        for k in range(6):
            row = sums_in[k // 2 : k // 2 + 1, :]
            if k % 2:
                row = pltpu.roll(row, feats, 1)
            weight_out[k : k + 1, :] = row[:, :feats]
        bias_out[...] = sums_in[3:4, :6]
        for copy in last:
            copy.start()
        for load, store in zip(loads, stores):
            load.wait()
            store.start()
        for copy in stores + last:
            copy.wait()

    return kernel


def inner_of(gx):
    return 8 if gx == 64 else 2


def per_device(features, head_weight, head_bias, probs, cotangent):
    zs, feats, nx, ny = features.shape
    chans = probs.shape[1]
    gx, gy = lax.axis_size("gx"), lax.axis_size("gy")
    inner = inner_of(gx)
    outer = gx // inner
    factor = 1.0 / math.sqrt(zs * nx * ny * gx * gy)
    dma = pltpu.SemaphoreType.DMA
    hbm = pl.BlockSpec(memory_space=pltpu.HBM)
    vmem = pl.BlockSpec(memory_space=pltpu.VMEM)
    field = pltpu.VMEM((ITERS, zs + 2, chans + 1, RING, ny), F32)
    coefs = pltpu.VMEM((zs + 2, 7, RING, ny), F32)
    grad_field, sums = pl.pallas_call(
        make_kernel(zs, chans, feats, gx, gy, inner, factor),
        out_shape=(
            jax.ShapeDtypeStruct(probs.shape, F32),
            jax.ShapeDtypeStruct((4, ny), F32),
        ),
        in_specs=[hbm, vmem, pl.BlockSpec(memory_space=pltpu.SMEM), hbm, hbm],
        out_specs=(hbm, vmem),
        scratch_shapes=[
            pltpu.VMEM((zs, feats * nx, ny), BF16),
            field,
            field,
            pltpu.VMEM((zs, chans, nx, ny), F32),
            coefs,
            coefs,
            pltpu.VMEM((zs, 6, nx, ny), F32),
            pltpu.VMEM((zs, nx, ny), F32),
            pltpu.VMEM((zs, 6 * nx, ny), BF16),
            pltpu.VMEM((6, nx, ny), F32),
            pltpu.VMEM((6 * nx, feats * nx), BF16),
            pltpu.VMEM((ny, 6 * ny), F32),
            pltpu.VMEM((3, zs, RING, ny), F32),
            pltpu.VMEM((3, zs, RING, ny), F32),
            pltpu.VMEM((zs * RING, ny), F32),
            pltpu.VMEM((2, zs, chans, nx, ny), F32),
            pltpu.VMEM((2, zs, 6, nx, ny), F32),
            pltpu.VMEM((gy, 4, ny), F32),
            pltpu.VMEM((inner, 4, ny), F32),
            pltpu.VMEM((outer, 4, ny), F32),
            dma((3 + zs,)),
            dma((5, 2)),
            dma((5, 2)),
            dma((2, len(SIDES))),
            dma((2, len(SIDES))),
            dma((gy - 1,)),
            dma((gy - 1,)),
            dma((inner - 1,)),
            dma((inner - 1,)),
            dma((outer - 1,)),
            dma((outer - 1,)),
        ],
        compiler_params=pltpu.CompilerParams(
            collective_id=0, has_side_effects=True, vmem_limit_bytes=63 * 1024 * 1024
        ),
        name="spread_backward",
    )(features.reshape(zs, feats * nx, ny), head_weight, head_bias, probs, cotangent)
    grad_probs, grad_weight, grad_bias = pl.pallas_call(
        deliver(feats),
        out_shape=(
            jax.ShapeDtypeStruct(probs.shape, F32),
            jax.ShapeDtypeStruct((6, feats), F32),
            jax.ShapeDtypeStruct((1, 6), F32),
        ),
        in_specs=[hbm, hbm],
        out_specs=(hbm, hbm, hbm),
        scratch_shapes=[
            pltpu.VMEM(probs.shape, F32),
            pltpu.VMEM((4, ny), F32),
            pltpu.VMEM((6, feats), F32),
            pltpu.VMEM((1, 6), F32),
            dma((2, zs)),
            dma((3,)),
        ],
        name="deliver",
    )(grad_field, sums)
    return grad_probs, grad_weight, grad_bias.reshape(6)


def solution(mesh):
    spec = P(None, None, "gx", "gy")
    return jax.shard_map(
        per_device,
        mesh=mesh,
        in_specs=(spec, P(), P(), spec, spec),
        out_specs=(spec, P(), P()),
        check_vma=False,
    )
```

```python
import math

import jax
import jax.numpy as jnp
from jax import lax
from jax.experimental import pallas as pl
from jax.experimental.pallas import tpu as pltpu
from jax.sharding import PartitionSpec as P

F32 = jnp.float32
BF16 = jnp.bfloat16
MESH = pl.DeviceIdType.MESH
ITERS = 3
NX, NY = 8, 128
RING = 16
EDGE = 16
LOW, HIGH = 3, 12
SIDES = [(dx, dy) for dx in (1, -1, 0) for dy in (0, 1, -1) if dx or dy]


def iota(shape, dim):
    return lax.broadcasted_iota(jnp.int32, shape, dim)


def rows_of(dx, count):
    if dx == 0:
        return pl.ds(0, NX), pl.ds(0, NX)
    if dx > 0:
        return pl.ds(NX - count, count), pl.ds(RING - count, count)
    return pl.ds(0, count), pl.ds(NX, count)


def make_kernel(zs, chans, feats, gx, gy, inner, factor):
    outer = gx // inner
    inside = pl.ds(1, zs)

    def kernel(
        feat_hbm, weight_ref, bias_ref, probs_hbm, cot_hbm,
        out_hbm, sum_ref,
        feat, hs, gs, g_out, kap, kst, act, inv, dlow, bias_acc, wide, expand,
        sf, sk, flat, far_g, far_k, sum_a, sum_b, sum_c,
        local_sem, row_send, row_recv, strip_send, strip_recv,
        sa_sem, ra_sem, sb_sem, rb_sem, sc_sem, rc_sem,
    ):
        me_x, me_y = lax.axis_index("gx"), lax.axis_index("gy")
        me_in, me_out = lax.rem(me_x, inner), lax.div(me_x, inner)

        def at(dx, dy):
            return lax.rem(me_x + dx + gx, gx), lax.rem(me_y + dy + gy, gy)

        partners_a = [(me_x, lax.rem(me_y + d, gy)) for d in range(1, gy)]
        partners_b = [(me_out * inner + lax.rem(me_in + d, inner), me_y) for d in range(1, inner)]
        partners_c = [(lax.rem(me_out + d, outer) * inner + me_in, me_y) for d in range(1, outer)]
        greeted = [at(dx, dy) for dx, dy in SIDES if dx] + partners_a + partners_b + partners_c
        fields_in = [
            pltpu.make_async_copy(source, field.at[0, inside, pl.ds(0, chans), pl.ds(0, NX)], local_sem.at[i])
            for i, (source, field) in enumerate(((probs_hbm, hs), (cot_hbm, gs)))
        ]
        feats_in = [
            pltpu.make_async_copy(feat_hbm.at[z], feat.at[z], local_sem.at[2 + z]) for z in range(zs)
        ]
        for load in fields_in:
            load.start()
        barrier = pltpu.get_barrier_semaphore()
        for partner in greeted:
            pl.semaphore_signal(barrier, inc=1, device_id=partner, device_id_type=MESH)
        for load in feats_in:
            load.start()

        for field in (hs, gs):
            for step in range(ITERS):
                for z in (0, zs + 1):
                    field[step, z] = jnp.zeros((chans + 1, RING, NY), F32)
        for coefs in (kap, kst):
            for z in (0, zs + 1):
                coefs[z] = jnp.zeros((7, RING, NY), F32)

        spread = (iota((feats, feats * NX), 1) >> 3) == iota((feats, feats * NX), 0)
        same_x = (iota((6 * NX, feats * NX), 1) & 7) == (iota((6 * NX, feats * NX), 0) & 7)
        weight = weight_ref[...].astype(F32)
        rows = jnp.concatenate(
            [jnp.broadcast_to(weight[k : k + 1, :], (NX, feats)) for k in range(6)], axis=0
        )
        tall = jnp.dot(
            rows.astype(BF16), spread.astype(F32).astype(BF16), preferred_element_type=F32
        )
        wide[...] = jnp.where(same_x, tall, 0.0).astype(BF16)
        here, there = iota((NY, 6 * NY), 0), iota((NY, 6 * NY), 1)
        expand[...] = (((here >> 4) == (there >> 7)) & ((here & 15) == (there & 15))).astype(F32)

        lane = iota((NX, NY), 1)
        lane_j = lane & (EDGE - 1)
        ring_lane = iota((RING, NY), 1)
        ring_j = ring_lane & (EDGE - 1)
        ring_row = iota((RING, NY), 0)
        has_right, has_left = me_x < gx - 1, me_x > 0
        has_up, has_down = me_y < gy - 1, me_y > 0

        def packed(values):
            tile = jnp.zeros((NX, NY), F32)
            for i, value in enumerate(values):
                tile = jnp.where((lane >> 4) == i, pltpu.roll(value, i * EDGE + 4, 1), tile)
            return jnp.where(lane_j < 8, tile, 0.0)

        def unpacked(own, low, high, first):
            seen = (
                (ring_row < NX) | ((ring_row < NX + 4) & has_right) | ((ring_row >= NX + 4) & has_left)
            )
            low = jnp.where(has_down, low, 0.0)
            high = jnp.where(has_up, high, 0.0)
            near = jnp.where(ring_j < first + 4, low, own)
            far = jnp.where(ring_j < first + 4, own, high)
            if first:
                near = pltpu.roll(near, NY - first, 1)
            else:
                far = pltpu.roll(far, 8, 1)
            return jnp.where(seen, jnp.where(ring_j < 8, near, far), 0.0)

        def over_z(body):
            def run(z, carry):
                body(z)
                return carry

            lax.fori_loop(0, zs, run, 0, unroll=True)

        def remote(source, target, send_sem, recv_sem, device):
            return pltpu.make_async_remote_copy(
                src_ref=source, dst_ref=target, send_sem=send_sem, recv_sem=recv_sem,
                device_id=device, device_id_type=MESH,
            )

        pending, arriving = [], []

        def send(copies, awaited=True):
            for copy in copies:
                copy.start()
            pending.extend(copies)
            if awaited:
                arriving.extend(copies)
            return copies

        def row_copies(which, count, view):
            return [
                remote(
                    view(rows_of(dx, count)[0]), view(rows_of(dx, count)[1]),
                    row_send.at[which, i], row_recv.at[which, i], at(dx, 0),
                )
                for i, dx in enumerate((1, -1))
            ]

        def far_copies(which, view, target):
            return [
                remote(
                    view(pl.ds(row, 1)), target.at[i, pl.ds(0, zs), pl.ds(0, target.shape[2]), pl.ds(0, 1)],
                    row_send.at[which, i], row_recv.at[which, i], at(dx, 0),
                )
                for i, (dx, row) in enumerate(((1, NX - 3), (-1, 2)))
            ]

        def strip_copies(which, strip):
            return [
                remote(
                    strip.at[0, pl.ds(0, zs), rows_of(dx, 3)[0]],
                    strip.at[(0, 1, 2)[dy], pl.ds(0, zs), rows_of(dx, 3)[1]],
                    strip_send.at[which, i], strip_recv.at[which, i], at(dx, dy),
                )
                for i, (dx, dy) in enumerate(SIDES)
            ]

        for load in fields_in:
            load.wait()

        def pack_fields(z):
            of_h = packed([hs[0, z + 1, c, :NX] for c in range(chans)])
            of_g = packed([gs[0, z + 1, c, :NX] for c in range(chans)])
            sf[0, z, :NX] = of_h + pltpu.roll(of_g, 8, 1)

        over_z(pack_fields)
        pl.semaphore_wait(barrier, len(greeted))
        g_rows = lambda r: gs.at[0, inside, pl.ds(0, chans), r]
        k_rows = lambda r: kap.at[inside, pl.ds(0, 6), r]
        send(row_copies(0, 3, lambda r: hs.at[0, inside, pl.ds(0, chans), r]))
        send(row_copies(1, 2, g_rows))
        send(strip_copies(0, sf))

        biases = [bias_ref[k] for k in range(6)]
        for load in feats_in:
            load.wait()

        def head(z):
            logits = jnp.dot(wide[...], feat[z], preferred_element_type=F32)
            active = [jax.nn.sigmoid(logits[k * NX : (k + 1) * NX] + biases[k]) for k in range(6)]
            summed = active[0]
            for k in range(1, 6):
                summed = summed + active[k]
            inverse = 1.0 / (summed + 1.0)
            coupling = [active[k] * inverse for k in range(6)]
            for k in range(6):
                act[z, k] = active[k]
                kap[z + 1, k, :NX] = coupling[k]
            inv[z] = inverse
            sk[0, z, :NX] = packed(coupling)

        over_z(head)
        send(row_copies(2, 2, k_rows))
        send(strip_copies(1, sk))
        outermost = send(far_copies(3, g_rows, far_g) + far_copies(4, k_rows, far_k), awaited=False)
        for copy in arriving:
            copy.wait_recv()

        def clear(rows):
            hs[0, 1 : zs + 1, :chans, rows] = jnp.zeros((zs, chans, 4, NY), F32)
            kap[1 : zs + 1, :6, rows] = jnp.zeros((zs, 6, 4, NY), F32)

        @pl.when(me_x == gx - 1)
        def _():
            clear(slice(NX, NX + 4))

        @pl.when(me_x == 0)
        def _():
            clear(slice(NX + 4, RING))

        def assemble(z):
            hs[0, z + 1, chans] = unpacked(sf[0, z], sf[1, z], sf[2, z], 0)
            gs[0, z + 1, chans] = unpacked(sf[0, z], sf[1, z], sf[2, z], 8)
            flat[pl.ds(z * RING, RING)] = unpacked(sk[0, z], sk[1, z], sk[2, z], 0)

        over_z(assemble)
        strips = jnp.dot(
            flat[...], expand[...], precision=lax.Precision.HIGHEST, preferred_element_type=F32
        )
        for z in range(zs):
            for coefs, value in (
                (kst, [strips[z * RING : (z + 1) * RING, k * NY : (k + 1) * NY] for k in range(6)]),
                (kap, [kap[z + 1, k] for k in range(6)]),
            ):
                centre = 1.0
                for k in range(6):
                    centre = centre - value[k]
                    if coefs is kst:
                        coefs[z + 1, k] = value[k]
                coefs[z + 1, 6] = centre

        def columns(strip, j):
            return jnp.stack(
                [
                    jnp.broadcast_to(strip[:, c * EDGE + j : c * EDGE + j + 1], strip.shape)
                    for c in range(chans)
                ]
            )

        def around(rnd, z, rows):
            h, strip = hs[rnd, z + 1, :chans], hs[rnd, z + 1, chans, :rows]
            shape = (chans, rows, NY)
            lanes = iota(shape, 2)
            centre = h[:, :rows]
            return centre, [
                pltpu.roll(h, RING - 1, 1)[:, :rows],
                pltpu.roll(h, 1, 1)[:, :rows],
                jnp.where(lanes == NY - 1, columns(strip, HIGH), pltpu.roll(centre, NY - 1, 2)),
                jnp.where(lanes == 0, columns(strip, LOW), pltpu.roll(centre, 1, 2)),
                hs[rnd, z + 2, :chans, :rows],
                hs[rnd, z, :chans, :rows],
            ]

        def forward(rnd, z):
            h, beside = around(rnd, z, RING)
            result = kap[z + 1, 6] * h
            for k in range(6):
                result = result + kap[z + 1, k] * beside[k]
            strip = hs[rnd, z + 1, chans]
            edge = kst[z + 1, 6] * strip
            for k, value in enumerate((
                pltpu.roll(strip, RING - 1, 0),
                pltpu.roll(strip, 1, 0),
                pltpu.roll(strip, NY - 1, 1),
                pltpu.roll(strip, 1, 1),
                hs[rnd, z + 2, chans],
                hs[rnd, z, chans],
            )):
                edge = edge + kst[z + 1, k] * value
            hs[rnd + 1, z + 1, :chans] = result
            hs[rnd + 1, z + 1, chans] = edge

        def backward(rnd, z, rows):
            g, strip = gs[rnd, z + 1, :chans], gs[rnd, z + 1, chans]
            lanes = iota((chans, rows, NY), 2)
            near = g[:, :rows]
            edge = [kst[z + 1, k] * strip for k in range(4)]
            result = kap[z + 1, 6, :rows] * near
            result = result + pltpu.roll(kap[z + 1, 0] * g, 1, 1)[:, :rows]
            result = result + pltpu.roll(kap[z + 1, 1] * g, RING - 1, 1)[:, :rows]
            result = result + jnp.where(
                lanes == 0,
                columns(edge[2][:rows], LOW),
                pltpu.roll(kap[z + 1, 2, :rows] * near, 1, 2),
            )
            result = result + jnp.where(
                lanes == NY - 1,
                columns(edge[3][:rows], HIGH),
                pltpu.roll(kap[z + 1, 3, :rows] * near, NY - 1, 2),
            )
            result = result + kap[z, 4, :rows] * gs[rnd, z, :chans, :rows]
            result = result + kap[z + 2, 5, :rows] * gs[rnd, z + 2, :chans, :rows]
            if rows == NX:
                return result
            strip = kst[z + 1, 6] * strip
            strip = strip + pltpu.roll(edge[0], 1, 0) + pltpu.roll(edge[1], RING - 1, 0)
            strip = strip + pltpu.roll(edge[2], 1, 1) + pltpu.roll(edge[3], NY - 1, 1)
            strip = strip + kst[z, 4] * gs[rnd, z, chans] + kst[z + 2, 5] * gs[rnd, z + 2, chans]
            gs[rnd + 1, z + 1, :chans] = result
            gs[rnd + 1, z + 1, chans] = strip

        for rnd in range(ITERS - 1):

            def advance(z, rnd=rnd):
                forward(rnd, z)
                backward(rnd, z, RING)

            over_z(advance)

        bias_acc[...] = jnp.zeros((6, NX, NY), F32)

        def slopes(z):
            parts = [jnp.zeros((NX, NY), F32) for _ in range(7)]
            for rnd in range(ITERS):
                g = gs[ITERS - 1 - rnd, z + 1, :chans, :NX]
                h, beside = around(rnd, z, NX)
                for k in range(6):
                    parts[k] = parts[k] + jnp.sum(g * beside[k], 0)
                parts[6] = parts[6] + jnp.sum(g * h, 0)
            inner_sum = jnp.zeros((NX, NY), F32)
            effective = []
            for k in range(6):
                value = parts[k] - parts[6]
                effective.append(value)
                inner_sum = inner_sum + value * kap[z + 1, k, :NX]
            pieces = []
            for k in range(6):
                active = act[z, k]
                slope = (effective[k] - inner_sum) * inv[z] * active * (1.0 - active)
                bias_acc[k] += slope
                pieces.append(slope)
            dlow[z] = jnp.concatenate(pieces, axis=0).astype(BF16)

        over_z(slopes)

        cells = feats * NX
        total = jnp.zeros((cells, 6 * NX), F32)
        for z in range(0, zs, 2):
            total = total + lax.dot_general(
                jnp.concatenate([feat[z], feat[z + 1]], axis=1),
                jnp.concatenate([dlow[z], dlow[z + 1]], axis=1),
                (((1,), (1,)), ((), ())),
                preferred_element_type=F32,
            )
        total = jnp.where((iota((cells, 6 * NX), 0) & 7) == (iota((cells, 6 * NX), 1) & 7), total, 0.0)
        over_f = ((iota((2 * feats, cells), 1) >> 3) == iota((2 * feats, cells), 0)).astype(F32)
        over_k = ((iota((8, 6 * NX), 1) >> 3) == iota((8, 6 * NX), 0)).astype(F32)
        by_f = jnp.dot(over_f, total, precision=lax.Precision.HIGHEST, preferred_element_type=F32)
        by_f = lax.dot_general(
            over_k, by_f, (((1,), (1,)), ((), ())),
            precision=lax.Precision.HIGHEST, preferred_element_type=F32,
        )
        lane_row = iota((1, NY), 1)
        payload = [
            jnp.where(
                lane_row < feats,
                by_f[2 * r : 2 * r + 1],
                pltpu.roll(by_f[2 * r + 1 : 2 * r + 2], feats, 1),
            )
            for r in range(3)
        ]
        bias_row = jnp.zeros((1, NY), F32)
        for k in range(6):
            amount = jnp.sum(jnp.sum(bias_acc[k], 0, keepdims=True), 1, keepdims=True)
            bias_row = jnp.where(lane_row == k, amount, bias_row)
        payload = jnp.concatenate(payload + [bias_row], axis=0)

        def exchange(buffer, me, partners, send_sem, recv_sem, value):
            buffer[me] = value
            copies = [
                remote(buffer.at[me], buffer.at[me], send_sem.at[d], recv_sem.at[d], partner)
                for d, partner in enumerate(partners)
            ]
            for copy in copies:
                copy.start()
            pending.extend(copies)
            return copies

        def gather(buffer, copies, count):
            for copy in copies:
                copy.wait_recv()
            value = buffer[0]
            for i in range(1, count):
                value = value + buffer[i]
            return value

        first = exchange(sum_a, me_y, partners_a, sa_sem, ra_sem, payload)

        for copy in outermost:
            copy.wait_recv()

        def widen(z):
            for i, (known, row) in enumerate(((has_left, RING - 3), (has_right, NX + 2))):
                gs[0, z + 1, :chans, row : row + 1] = far_g[i, z, :, :1]
                kap[z + 1, :6, row : row + 1] = jnp.where(known, far_k[i, z, :, :1], 0.0)
            centre = 1.0
            for k in range(6):
                centre = centre - kap[z + 1, k, NX:]
            kap[z + 1, 6, NX:] = centre

        over_z(widen)
        for rnd in range(ITERS - 1):
            over_z(lambda z, rnd=rnd: backward(rnd, z, RING))

        def finish(z):
            g_out[z] = backward(ITERS - 1, z, NX)

        over_z(finish)
        store = pltpu.make_async_copy(g_out, out_hbm, local_sem.at[2 + zs])
        store.start()

        value = gather(sum_a, first, gy)
        second = exchange(sum_b, me_in, partners_b, sb_sem, rb_sem, value)
        value = gather(sum_b, second, inner)
        third = exchange(sum_c, me_out, partners_c, sc_sem, rc_sem, value)
        sum_ref[...] = gather(sum_c, third, outer) * factor
        for copy in pending:
            copy.wait_send()
        store.wait()

    return kernel


def deliver(feats):
    def kernel(field, sums, grad_probs, grad_weight, grad_bias, held, sums_in, weight_out, bias_out, sems, small):
        planes = range(field.shape[0])
        loads = [pltpu.make_async_copy(field.at[z], held.at[z], sems.at[0, z]) for z in planes]
        stores = [pltpu.make_async_copy(held.at[z], grad_probs.at[z], sems.at[1, z]) for z in planes]
        first = pltpu.make_async_copy(sums, sums_in, small.at[0])
        last = [
            pltpu.make_async_copy(weight_out, grad_weight, small.at[1]),
            pltpu.make_async_copy(bias_out, grad_bias, small.at[2]),
        ]
        first.start()
        for load in loads:
            load.start()
        first.wait()
        for k in range(6):
            row = sums_in[k // 2 : k // 2 + 1, :]
            if k % 2:
                row = pltpu.roll(row, feats, 1)
            weight_out[k : k + 1, :] = row[:, :feats]
        bias_out[...] = sums_in[3:4, :6]
        for copy in last:
            copy.start()
        for load, store in zip(loads, stores):
            load.wait()
            store.start()
        for copy in stores + last:
            copy.wait()

    return kernel


def inner_of(gx):
    return 8 if gx == 64 else 2


def per_device(features, head_weight, head_bias, probs, cotangent):
    zs, feats, nx, ny = features.shape
    chans = probs.shape[1]
    gx, gy = lax.axis_size("gx"), lax.axis_size("gy")
    inner = inner_of(gx)
    outer = gx // inner
    factor = 1.0 / math.sqrt(zs * nx * ny * gx * gy)
    dma = pltpu.SemaphoreType.DMA
    hbm = pl.BlockSpec(memory_space=pltpu.HBM)
    vmem = pl.BlockSpec(memory_space=pltpu.VMEM)
    field = pltpu.VMEM((ITERS, zs + 2, chans + 1, RING, ny), F32)
    coefs = pltpu.VMEM((zs + 2, 7, RING, ny), F32)
    grad_field, sums = pl.pallas_call(
        make_kernel(zs, chans, feats, gx, gy, inner, factor),
        out_shape=(
            jax.ShapeDtypeStruct(probs.shape, F32),
            jax.ShapeDtypeStruct((4, ny), F32),
        ),
        in_specs=[hbm, vmem, pl.BlockSpec(memory_space=pltpu.SMEM), hbm, hbm],
        out_specs=(hbm, vmem),
        scratch_shapes=[
            pltpu.VMEM((zs, feats * nx, ny), BF16),
            field,
            field,
            pltpu.VMEM((zs, chans, nx, ny), F32),
            coefs,
            coefs,
            pltpu.VMEM((zs, 6, nx, ny), F32),
            pltpu.VMEM((zs, nx, ny), F32),
            pltpu.VMEM((zs, 6 * nx, ny), BF16),
            pltpu.VMEM((6, nx, ny), F32),
            pltpu.VMEM((6 * nx, feats * nx), BF16),
            pltpu.VMEM((ny, 6 * ny), F32),
            pltpu.VMEM((3, zs, RING, ny), F32),
            pltpu.VMEM((3, zs, RING, ny), F32),
            pltpu.VMEM((zs * RING, ny), F32),
            pltpu.VMEM((2, zs, chans, nx, ny), F32),
            pltpu.VMEM((2, zs, 6, nx, ny), F32),
            pltpu.VMEM((gy, 4, ny), F32),
            pltpu.VMEM((inner, 4, ny), F32),
            pltpu.VMEM((outer, 4, ny), F32),
            dma((3 + zs,)),
            dma((5, 2)),
            dma((5, 2)),
            dma((2, len(SIDES))),
            dma((2, len(SIDES))),
            dma((gy - 1,)),
            dma((gy - 1,)),
            dma((inner - 1,)),
            dma((inner - 1,)),
            dma((outer - 1,)),
            dma((outer - 1,)),
        ],
        compiler_params=pltpu.CompilerParams(
            collective_id=0, has_side_effects=True, vmem_limit_bytes=63 * 1024 * 1024
        ),
        name="spread_backward",
    )(features.reshape(zs, feats * nx, ny), head_weight, head_bias, probs, cotangent)
    grad_probs, grad_weight, grad_bias = pl.pallas_call(
        deliver(feats),
        out_shape=(
            jax.ShapeDtypeStruct(probs.shape, F32),
            jax.ShapeDtypeStruct((6, feats), F32),
            jax.ShapeDtypeStruct((1, 6), F32),
        ),
        in_specs=[hbm, hbm],
        out_specs=(hbm, hbm, hbm),
        scratch_shapes=[
            pltpu.VMEM(probs.shape, F32),
            pltpu.VMEM((4, ny), F32),
            pltpu.VMEM((6, feats), F32),
            pltpu.VMEM((1, 6), F32),
            dma((2, zs)),
            dma((3,)),
        ],
        name="deliver",
    )(grad_field, sums)
    return grad_probs, grad_weight, grad_bias.reshape(6)


def solution(mesh):
    spec = P(None, None, "gx", "gy")
    return jax.shard_map(
        per_device,
        mesh=mesh,
        in_specs=(spec, P(), P(), spec, spec),
        out_specs=(spec, P(), P()),
        check_vma=False,
    )
```

```python
import math

import jax
import jax.numpy as jnp
from jax import lax
from jax.experimental import pallas as pl
from jax.experimental.pallas import tpu as pltpu
from jax.sharding import PartitionSpec as P

F32 = jnp.float32
BF16 = jnp.bfloat16
MESH = pl.DeviceIdType.MESH
ITERS = 3
NX, NY = 8, 128
RING = 16
EDGE = 16
LOW, HIGH = 3, 12
SIDES = [(dx, dy) for dx in (1, -1, 0) for dy in (0, 1, -1) if dx or dy]


def iota(shape, dim):
    return lax.broadcasted_iota(jnp.int32, shape, dim)


def rows_of(dx, count):
    if dx == 0:
        return pl.ds(0, NX), pl.ds(0, NX)
    if dx > 0:
        return pl.ds(NX - count, count), pl.ds(RING - count, count)
    return pl.ds(0, count), pl.ds(NX, count)


def make_kernel(zs, chans, feats, gx, gy, inner, factor):
    outer = gx // inner
    inside = pl.ds(1, zs)

    def kernel(
        feat_hbm, weight_ref, bias_ref, probs_hbm, cot_hbm,
        out_hbm, sum_ref,
        feat, hs, gs, g_out, kap, kst, act, inv, dlow, bias_acc, wide, expand,
        sf, sk, flat, far_g, far_k, sum_a, sum_b, sum_c,
        local_sem, row_send, row_recv, strip_send, strip_recv,
        sa_sem, ra_sem, sb_sem, rb_sem, sc_sem, rc_sem,
    ):
        me_x, me_y = lax.axis_index("gx"), lax.axis_index("gy")
        me_in, me_out = lax.rem(me_x, inner), lax.div(me_x, inner)

        def at(dx, dy):
            return lax.rem(me_x + dx + gx, gx), lax.rem(me_y + dy + gy, gy)

        partners_a = [(me_x, lax.rem(me_y + d, gy)) for d in range(1, gy)]
        partners_b = [(me_out * inner + lax.rem(me_in + d, inner), me_y) for d in range(1, inner)]
        partners_c = [(lax.rem(me_out + d, outer) * inner + me_in, me_y) for d in range(1, outer)]
        greeted = [at(dx, dy) for dx, dy in SIDES if dx] + partners_a + partners_b + partners_c
        fields_in = [
            pltpu.make_async_copy(source, field.at[0, inside, pl.ds(0, chans), pl.ds(0, NX)], local_sem.at[i])
            for i, (source, field) in enumerate(((probs_hbm, hs), (cot_hbm, gs)))
        ]
        feats_in = [
            pltpu.make_async_copy(feat_hbm.at[z], feat.at[z], local_sem.at[2 + z]) for z in range(zs)
        ]
        for load in fields_in:
            load.start()
        barrier = pltpu.get_barrier_semaphore()
        for partner in greeted:
            pl.semaphore_signal(barrier, inc=1, device_id=partner, device_id_type=MESH)
        for load in feats_in:
            load.start()

        for field in (hs, gs):
            for step in range(ITERS):
                for z in (0, zs + 1):
                    field[step, z] = jnp.zeros((chans + 1, RING, NY), F32)
        for coefs in (kap, kst):
            for z in (0, zs + 1):
                coefs[z] = jnp.zeros((7, RING, NY), F32)

        spread = (iota((feats, feats * NX), 1) >> 3) == iota((feats, feats * NX), 0)
        same_x = (iota((6 * NX, feats * NX), 1) & 7) == (iota((6 * NX, feats * NX), 0) & 7)
        weight = weight_ref[...].astype(F32)
        rows = jnp.concatenate(
            [jnp.broadcast_to(weight[k : k + 1, :], (NX, feats)) for k in range(6)], axis=0
        )
        tall = jnp.dot(
            rows.astype(BF16), spread.astype(F32).astype(BF16), preferred_element_type=F32
        )
        wide[...] = jnp.where(same_x, tall, 0.0).astype(BF16)
        here, there = iota((NY, 6 * NY), 0), iota((NY, 6 * NY), 1)
        expand[...] = (((here >> 4) == (there >> 7)) & ((here & 15) == (there & 15))).astype(F32)

        lane = iota((NX, NY), 1)
        lane_j = lane & (EDGE - 1)
        ring_lane = iota((RING, NY), 1)
        ring_j = ring_lane & (EDGE - 1)
        ring_row = iota((RING, NY), 0)
        has_right, has_left = me_x < gx - 1, me_x > 0
        has_up, has_down = me_y < gy - 1, me_y > 0

        def packed(values):
            tile = jnp.zeros((NX, NY), F32)
            for i, value in enumerate(values):
                tile = jnp.where((lane >> 4) == i, pltpu.roll(value, i * EDGE + 4, 1), tile)
            return jnp.where(lane_j < 8, tile, 0.0)

        def unpacked(own, low, high, first):
            seen = (
                (ring_row < NX) | ((ring_row < NX + 4) & has_right) | ((ring_row >= NX + 4) & has_left)
            )
            low = jnp.where(has_down, low, 0.0)
            high = jnp.where(has_up, high, 0.0)
            near = jnp.where(ring_j < first + 4, low, own)
            far = jnp.where(ring_j < first + 4, own, high)
            if first:
                near = pltpu.roll(near, NY - first, 1)
            else:
                far = pltpu.roll(far, 8, 1)
            return jnp.where(seen, jnp.where(ring_j < 8, near, far), 0.0)

        def over_z(body):
            def run(z, carry):
                body(z)
                return carry

            lax.fori_loop(0, zs, run, 0, unroll=True)

        def remote(source, target, send_sem, recv_sem, device):
            return pltpu.make_async_remote_copy(
                src_ref=source, dst_ref=target, send_sem=send_sem, recv_sem=recv_sem,
                device_id=device, device_id_type=MESH,
            )

        pending, arriving = [], []

        def send(copies, awaited=True):
            for copy in copies:
                copy.start()
            pending.extend(copies)
            if awaited:
                arriving.extend(copies)
            return copies

        def row_copies(which, count, view):
            return [
                remote(
                    view(rows_of(dx, count)[0]), view(rows_of(dx, count)[1]),
                    row_send.at[which, i], row_recv.at[which, i], at(dx, 0),
                )
                for i, dx in enumerate((1, -1))
            ]

        def far_copies(which, view, target):
            return [
                remote(
                    view(pl.ds(row, 1)), target.at[i, pl.ds(0, zs), pl.ds(0, target.shape[2]), pl.ds(0, 1)],
                    row_send.at[which, i], row_recv.at[which, i], at(dx, 0),
                )
                for i, (dx, row) in enumerate(((1, NX - 3), (-1, 2)))
            ]

        def strip_copies(which, strip):
            return [
                remote(
                    strip.at[0, pl.ds(0, zs), rows_of(dx, 3)[0]],
                    strip.at[(0, 1, 2)[dy], pl.ds(0, zs), rows_of(dx, 3)[1]],
                    strip_send.at[which, i], strip_recv.at[which, i], at(dx, dy),
                )
                for i, (dx, dy) in enumerate(SIDES)
            ]

        for load in fields_in:
            load.wait()

        def pack_fields(z):
            of_h = packed([hs[0, z + 1, c, :NX] for c in range(chans)])
            of_g = packed([gs[0, z + 1, c, :NX] for c in range(chans)])
            sf[0, z, :NX] = of_h + pltpu.roll(of_g, 8, 1)

        over_z(pack_fields)
        pl.semaphore_wait(barrier, len(greeted))
        g_rows = lambda r: gs.at[0, inside, pl.ds(0, chans), r]
        k_rows = lambda r: kap.at[inside, pl.ds(0, 6), r]
        send(row_copies(0, 3, lambda r: hs.at[0, inside, pl.ds(0, chans), r]))
        send(row_copies(1, 2, g_rows))
        send(strip_copies(0, sf))

        biases = [bias_ref[k] for k in range(6)]
        for load in feats_in:
            load.wait()

        def head(z):
            logits = jnp.dot(wide[...], feat[z], preferred_element_type=F32)
            active = [jax.nn.sigmoid(logits[k * NX : (k + 1) * NX] + biases[k]) for k in range(6)]
            summed = active[0]
            for k in range(1, 6):
                summed = summed + active[k]
            inverse = 1.0 / (summed + 1.0)
            coupling = [active[k] * inverse for k in range(6)]
            for k in range(6):
                act[z, k] = active[k]
                kap[z + 1, k, :NX] = coupling[k]
            inv[z] = inverse
            sk[0, z, :NX] = packed(coupling)

        over_z(head)
        send(row_copies(2, 2, k_rows))
        send(strip_copies(1, sk))
        outermost = send(far_copies(3, g_rows, far_g) + far_copies(4, k_rows, far_k), awaited=False)
        for copy in arriving:
            copy.wait_recv()

        def clear(rows):
            hs[0, 1 : zs + 1, :chans, rows] = jnp.zeros((zs, chans, 4, NY), F32)
            kap[1 : zs + 1, :6, rows] = jnp.zeros((zs, 6, 4, NY), F32)

        @pl.when(me_x == gx - 1)
        def _():
            clear(slice(NX, NX + 4))

        @pl.when(me_x == 0)
        def _():
            clear(slice(NX + 4, RING))

        def assemble(z):
            hs[0, z + 1, chans] = unpacked(sf[0, z], sf[1, z], sf[2, z], 0)
            gs[0, z + 1, chans] = unpacked(sf[0, z], sf[1, z], sf[2, z], 8)
            flat[pl.ds(z * RING, RING)] = unpacked(sk[0, z], sk[1, z], sk[2, z], 0)

        over_z(assemble)
        strips = jnp.dot(
            flat[...], expand[...], precision=lax.Precision.HIGHEST, preferred_element_type=F32
        )
        for z in range(zs):
            for coefs, value in (
                (kst, [strips[z * RING : (z + 1) * RING, k * NY : (k + 1) * NY] for k in range(6)]),
                (kap, [kap[z + 1, k] for k in range(6)]),
            ):
                centre = 1.0
                for k in range(6):
                    centre = centre - value[k]
                    if coefs is kst:
                        coefs[z + 1, k] = value[k]
                coefs[z + 1, 6] = centre

        def columns(strip, j):
            return jnp.stack(
                [
                    jnp.broadcast_to(strip[:, c * EDGE + j : c * EDGE + j + 1], strip.shape)
                    for c in range(chans)
                ]
            )

        def around(rnd, z, rows):
            h, strip = hs[rnd, z + 1, :chans], hs[rnd, z + 1, chans, :rows]
            shape = (chans, rows, NY)
            lanes = iota(shape, 2)
            centre = h[:, :rows]
            return centre, [
                pltpu.roll(h, RING - 1, 1)[:, :rows],
                pltpu.roll(h, 1, 1)[:, :rows],
                jnp.where(lanes == NY - 1, columns(strip, HIGH), pltpu.roll(centre, NY - 1, 2)),
                jnp.where(lanes == 0, columns(strip, LOW), pltpu.roll(centre, 1, 2)),
                hs[rnd, z + 2, :chans, :rows],
                hs[rnd, z, :chans, :rows],
            ]

        def forward(rnd, z):
            h, beside = around(rnd, z, RING)
            result = kap[z + 1, 6] * h
            for k in range(6):
                result = result + kap[z + 1, k] * beside[k]
            strip = hs[rnd, z + 1, chans]
            edge = kst[z + 1, 6] * strip
            for k, value in enumerate((
                pltpu.roll(strip, RING - 1, 0),
                pltpu.roll(strip, 1, 0),
                pltpu.roll(strip, NY - 1, 1),
                pltpu.roll(strip, 1, 1),
                hs[rnd, z + 2, chans],
                hs[rnd, z, chans],
            )):
                edge = edge + kst[z + 1, k] * value
            hs[rnd + 1, z + 1, :chans] = result
            hs[rnd + 1, z + 1, chans] = edge

        def backward(rnd, z, rows):
            g, strip = gs[rnd, z + 1, :chans], gs[rnd, z + 1, chans]
            lanes = iota((chans, rows, NY), 2)
            near = g[:, :rows]
            edge = [kst[z + 1, k] * strip for k in range(4)]
            result = kap[z + 1, 6, :rows] * near
            result = result + pltpu.roll(kap[z + 1, 0] * g, 1, 1)[:, :rows]
            result = result + pltpu.roll(kap[z + 1, 1] * g, RING - 1, 1)[:, :rows]
            result = result + jnp.where(
                lanes == 0,
                columns(edge[2][:rows], LOW),
                pltpu.roll(kap[z + 1, 2, :rows] * near, 1, 2),
            )
            result = result + jnp.where(
                lanes == NY - 1,
                columns(edge[3][:rows], HIGH),
                pltpu.roll(kap[z + 1, 3, :rows] * near, NY - 1, 2),
            )
            result = result + kap[z, 4, :rows] * gs[rnd, z, :chans, :rows]
            result = result + kap[z + 2, 5, :rows] * gs[rnd, z + 2, :chans, :rows]
            if rows == NX:
                return result
            strip = kst[z + 1, 6] * strip
            strip = strip + pltpu.roll(edge[0], 1, 0) + pltpu.roll(edge[1], RING - 1, 0)
            strip = strip + pltpu.roll(edge[2], 1, 1) + pltpu.roll(edge[3], NY - 1, 1)
            strip = strip + kst[z, 4] * gs[rnd, z, chans] + kst[z + 2, 5] * gs[rnd, z + 2, chans]
            gs[rnd + 1, z + 1, :chans] = result
            gs[rnd + 1, z + 1, chans] = strip

        for rnd in range(ITERS - 1):

            def advance(z, rnd=rnd):
                forward(rnd, z)
                backward(rnd, z, RING)

            over_z(advance)

        bias_acc[...] = jnp.zeros((6, NX, NY), F32)

        def slopes(z):
            parts = [jnp.zeros((NX, NY), F32) for _ in range(7)]
            for rnd in range(ITERS):
                g = gs[ITERS - 1 - rnd, z + 1, :chans, :NX]
                h, beside = around(rnd, z, NX)
                for k in range(6):
                    parts[k] = parts[k] + jnp.sum(g * beside[k], 0)
                parts[6] = parts[6] + jnp.sum(g * h, 0)
            inner_sum = jnp.zeros((NX, NY), F32)
            effective = []
            for k in range(6):
                value = parts[k] - parts[6]
                effective.append(value)
                inner_sum = inner_sum + value * kap[z + 1, k, :NX]
            pieces = []
            for k in range(6):
                active = act[z, k]
                slope = (effective[k] - inner_sum) * inv[z] * active * (1.0 - active)
                bias_acc[k] += slope
                pieces.append(slope)
            dlow[z] = jnp.concatenate(pieces, axis=0).astype(BF16)

        over_z(slopes)

        cells = feats * NX
        total = jnp.zeros((cells, 6 * NX), F32)
        for z in range(0, zs, 2):
            total = total + lax.dot_general(
                jnp.concatenate([feat[z], feat[z + 1]], axis=1),
                jnp.concatenate([dlow[z], dlow[z + 1]], axis=1),
                (((1,), (1,)), ((), ())),
                preferred_element_type=F32,
            )
        total = jnp.where((iota((cells, 6 * NX), 0) & 7) == (iota((cells, 6 * NX), 1) & 7), total, 0.0)
        over_f = ((iota((2 * feats, cells), 1) >> 3) == iota((2 * feats, cells), 0)).astype(F32)
        over_k = ((iota((8, 6 * NX), 1) >> 3) == iota((8, 6 * NX), 0)).astype(F32)
        by_f = jnp.dot(over_f, total, precision=lax.Precision.HIGHEST, preferred_element_type=F32)
        by_f = lax.dot_general(
            over_k, by_f, (((1,), (1,)), ((), ())),
            precision=lax.Precision.HIGHEST, preferred_element_type=F32,
        )
        lane_row = iota((1, NY), 1)
        payload = [
            jnp.where(
                lane_row < feats,
                by_f[2 * r : 2 * r + 1],
                pltpu.roll(by_f[2 * r + 1 : 2 * r + 2], feats, 1),
            )
            for r in range(3)
        ]
        bias_row = jnp.zeros((1, NY), F32)
        for k in range(6):
            amount = jnp.sum(jnp.sum(bias_acc[k], 0, keepdims=True), 1, keepdims=True)
            bias_row = jnp.where(lane_row == k, amount, bias_row)
        payload = jnp.concatenate(payload + [bias_row], axis=0)

        def exchange(buffer, me, partners, send_sem, recv_sem, value):
            buffer[me] = value
            copies = [
                remote(buffer.at[me], buffer.at[me], send_sem.at[d], recv_sem.at[d], partner)
                for d, partner in enumerate(partners)
            ]
            for copy in copies:
                copy.start()
            pending.extend(copies)
            return copies

        def gather(buffer, copies, count):
            for copy in copies:
                copy.wait_recv()
            value = buffer[0]
            for i in range(1, count):
                value = value + buffer[i]
            return value

        first = exchange(sum_b, me_in, partners_b, sb_sem, rb_sem, payload)

        for copy in outermost:
            copy.wait_recv()

        def widen(z):
            for i, (known, row) in enumerate(((has_left, RING - 3), (has_right, NX + 2))):
                gs[0, z + 1, :chans, row : row + 1] = far_g[i, z, :, :1]
                kap[z + 1, :6, row : row + 1] = jnp.where(known, far_k[i, z, :, :1], 0.0)
            centre = 1.0
            for k in range(6):
                centre = centre - kap[z + 1, k, NX:]
            kap[z + 1, 6, NX:] = centre

        over_z(widen)
        for rnd in range(ITERS - 1):
            over_z(lambda z, rnd=rnd: backward(rnd, z, RING))

        def finish(z):
            g_out[z] = backward(ITERS - 1, z, NX)

        over_z(finish)
        store = pltpu.make_async_copy(g_out, out_hbm, local_sem.at[2 + zs])
        store.start()

        value = gather(sum_b, first, inner)
        second = exchange(sum_a, me_y, partners_a, sa_sem, ra_sem, value)
        value = gather(sum_a, second, gy)
        third = exchange(sum_c, me_out, partners_c, sc_sem, rc_sem, value)
        sum_ref[...] = gather(sum_c, third, outer) * factor
        for copy in pending:
            copy.wait_send()
        store.wait()

    return kernel


def deliver(feats):
    def kernel(field, sums, grad_probs, grad_weight, grad_bias, held, sums_in, weight_out, bias_out, sems, small):
        planes = range(field.shape[0])
        loads = [pltpu.make_async_copy(field.at[z], held.at[z], sems.at[0, z]) for z in planes]
        stores = [pltpu.make_async_copy(held.at[z], grad_probs.at[z], sems.at[1, z]) for z in planes]
        first = pltpu.make_async_copy(sums, sums_in, small.at[0])
        last = [
            pltpu.make_async_copy(weight_out, grad_weight, small.at[1]),
            pltpu.make_async_copy(bias_out, grad_bias, small.at[2]),
        ]
        first.start()
        for load in loads:
            load.start()
        first.wait()
        for k in range(6):
            row = sums_in[k // 2 : k // 2 + 1, :]
            if k % 2:
                row = pltpu.roll(row, feats, 1)
            weight_out[k : k + 1, :] = row[:, :feats]
        bias_out[...] = sums_in[3:4, :6]
        for copy in last:
            copy.start()
        for load, store in zip(loads, stores):
            load.wait()
            store.start()
        for copy in stores + last:
            copy.wait()

    return kernel


def inner_of(gx):
    return 8 if gx == 64 else 2


def per_device(features, head_weight, head_bias, probs, cotangent):
    zs, feats, nx, ny = features.shape
    chans = probs.shape[1]
    gx, gy = lax.axis_size("gx"), lax.axis_size("gy")
    inner = inner_of(gx)
    outer = gx // inner
    factor = 1.0 / math.sqrt(zs * nx * ny * gx * gy)
    dma = pltpu.SemaphoreType.DMA
    hbm = pl.BlockSpec(memory_space=pltpu.HBM)
    vmem = pl.BlockSpec(memory_space=pltpu.VMEM)
    field = pltpu.VMEM((ITERS, zs + 2, chans + 1, RING, ny), F32)
    coefs = pltpu.VMEM((zs + 2, 7, RING, ny), F32)
    grad_field, sums = pl.pallas_call(
        make_kernel(zs, chans, feats, gx, gy, inner, factor),
        out_shape=(
            jax.ShapeDtypeStruct(probs.shape, F32),
            jax.ShapeDtypeStruct((4, ny), F32),
        ),
        in_specs=[hbm, vmem, pl.BlockSpec(memory_space=pltpu.SMEM), hbm, hbm],
        out_specs=(hbm, vmem),
        scratch_shapes=[
            pltpu.VMEM((zs, feats * nx, ny), BF16),
            field,
            field,
            pltpu.VMEM((zs, chans, nx, ny), F32),
            coefs,
            coefs,
            pltpu.VMEM((zs, 6, nx, ny), F32),
            pltpu.VMEM((zs, nx, ny), F32),
            pltpu.VMEM((zs, 6 * nx, ny), BF16),
            pltpu.VMEM((6, nx, ny), F32),
            pltpu.VMEM((6 * nx, feats * nx), BF16),
            pltpu.VMEM((ny, 6 * ny), F32),
            pltpu.VMEM((3, zs, RING, ny), F32),
            pltpu.VMEM((3, zs, RING, ny), F32),
            pltpu.VMEM((zs * RING, ny), F32),
            pltpu.VMEM((2, zs, chans, nx, ny), F32),
            pltpu.VMEM((2, zs, 6, nx, ny), F32),
            pltpu.VMEM((gy, 4, ny), F32),
            pltpu.VMEM((inner, 4, ny), F32),
            pltpu.VMEM((outer, 4, ny), F32),
            dma((3 + zs,)),
            dma((5, 2)),
            dma((5, 2)),
            dma((2, len(SIDES))),
            dma((2, len(SIDES))),
            dma((gy - 1,)),
            dma((gy - 1,)),
            dma((inner - 1,)),
            dma((inner - 1,)),
            dma((outer - 1,)),
            dma((outer - 1,)),
        ],
        compiler_params=pltpu.CompilerParams(
            collective_id=0, has_side_effects=True, vmem_limit_bytes=63 * 1024 * 1024
        ),
        name="spread_backward",
    )(features.reshape(zs, feats * nx, ny), head_weight, head_bias, probs, cotangent)
    grad_probs, grad_weight, grad_bias = pl.pallas_call(
        deliver(feats),
        out_shape=(
            jax.ShapeDtypeStruct(probs.shape, F32),
            jax.ShapeDtypeStruct((6, feats), F32),
            jax.ShapeDtypeStruct((1, 6), F32),
        ),
        in_specs=[hbm, hbm],
        out_specs=(hbm, hbm, hbm),
        scratch_shapes=[
            pltpu.VMEM(probs.shape, F32),
            pltpu.VMEM((4, ny), F32),
            pltpu.VMEM((6, feats), F32),
            pltpu.VMEM((1, 6), F32),
            dma((2, zs)),
            dma((3,)),
        ],
        name="deliver",
    )(grad_field, sums)
    return grad_probs, grad_weight, grad_bias.reshape(6)


def solution(mesh):
    spec = P(None, None, "gx", "gy")
    return jax.shard_map(
        per_device,
        mesh=mesh,
        in_specs=(spec, P(), P(), spec, spec),
        out_specs=(spec, P(), P()),
        check_vma=False,
    )
```
